32 devices in a mesh: conf: 2 (over y), row: 4 (over z), col: 4 (over x, core).
Axes of the slice: x: 2, y: 2, z: 4, core: 2. Of those that a mesh axis runs over, the one named last changes fastest.
Arguments:
- pair_state: bfloat16 [512, 256, 128], P(('conf', 'row'), 'col'), parts along dimension 0, may hold values from -6 to 6
- token_kinds: int32 [512], P('conf'), parts along dimension 0, may hold values from 0 to 31
- first_type_table: bfloat16 [32, 128], replicated, may hold values from -3 to 3
- second_type_table: bfloat16 [32, 128], replicated, may hold values from -3 to 3
- alignment_state: bfloat16 [64, 16384], P(None, ('conf', 'row', 'col')), parts along dimension 1, may hold values from -6 to 6
- alignment_index: int32 [64, 512], P(None, ('conf', 'row', 'col')), parts along dimension 1, may hold values from 0 to 31
- alignment_table: bfloat16 [32, 32], replicated, may hold values from -3 to 3
- first_weight: bfloat16 [32, 32], replicated, may hold values from -1 to 1
- second_weight: bfloat16 [32, 32], replicated, may hold values from -1 to 1
- outer_product_weight: bfloat16 [1024, 128], replicated, may hold values from -1.5 to 1.5
- outer_product_bias: bfloat16 [128], replicated, may hold values from -4 to 4
- pair_block_mask: int32 [32, 16], P(('conf', 'row'), 'col'), parts along dimension 0, may hold values 0 or 1
- transition_gain: float32 [128], replicated, may hold values from 0.25 to 1.75
- transition_gate_up: bfloat16 [128, 1024], replicated, may hold values from -0.5 to 0.5
- transition_down: bfloat16 [512, 128], replicated, may hold values from -0.25 to 0.25
- distance_weight: bfloat16 [128, 64], replicated, may hold values from -0.5 to 0.5
- distance_bias: float32 [64], replicated, may hold values from -4 to 4
Outputs:
- pair_out: bfloat16 [512, 256, 128], P(('conf', 'row'), 'col'), parts along dimension 0
- distogram: bfloat16 [512, 16384], P(('conf', 'row'), 'col'), parts along dimension 0
The draws below stay inside these ranges and needn't reach their ends.
There are 2 independent parts, one for each index of `conf`. The reference program is written for one: setup_inputs(seed, part) draws one part's arguments, and reference() takes and returns one part's arrays. A program takes and returns all parts, laid end to end along the dimension named above; an argument that names none is the same for every part. Nothing has to cross between parts.
All inputs are finite; a program needn't handle non-finite values. No bound on the sum of `pair_block_mask` on one device may be relied on, other than what follows from the above.
Results may differ from the reference program's by a relative error of at most 0.0071.
Values may be sent and summed in bfloat16 or wider, within the bound.
No kernel may reach another device: no remote copies, remote signals or barrier semaphores. Data moves between devices by JAX's collectives and lax.ppermute only.
A program may use at most 64 MiB of HBM per device.

```python
import jax
import jax.numpy as jnp
from jax import lax

TOKEN_COUNT = 256
ALIGN_ROWS = 64
ALIGN_FEATURES = 32
C = 32
CZ = 128
HID = 512
BINS = 64
RESIDUE_KINDS = 32
MB = 16


def touch_ends(drawn, rng, least, top_value):
    longest = drawn.shape.index(max(drawn.shape))
    spots = []
    for shift in (0, 1):
        where = [jax.random.randint(jax.random.fold_in(rng, axis), (), 0, length) for axis, length in enumerate(drawn.shape)]
        where[longest] = (where[longest] + shift) % drawn.shape[longest]
        spots.append(tuple(where))
    return drawn.at[spots[0]].set(least).at[spots[1]].set(top_value)


def level_of(rng, extent, shards, smallest, top_value):
    loudness = 1.0
    for dim, parts in shards:
        draws = jax.random.uniform(jax.random.fold_in(jax.random.fold_in(rng, 6), dim), (parts,), jnp.float32, smallest / len(shards), top_value / len(shards))
        loudness = loudness * jnp.repeat(jnp.exp(draws), extent[dim] // parts).reshape((-1,) + (1,) * (len(extent) - 1 - dim))
    return loudness


def normal_values(rng, extent, scale, most, pieces=(), kind=jnp.bfloat16):
    array = jax.random.normal(rng, extent, jnp.float32) * scale
    if len(pieces) > 0:
        array = level_of(rng, extent, pieces, -0.22, 0.18) * array
    return jnp.clip(array, min=-most, max=most).astype(kind)


def setup_inputs(seed: int = 0, part: int = 0) -> dict:
    keys = jax.random.split(jax.random.key(seed), 18)
    own_keys = jax.random.split(jax.random.fold_in(keys[17], part), 18)
    return {
        "pair_state": normal_values(own_keys[0], (TOKEN_COUNT, TOKEN_COUNT, CZ), 1.0, 6.0, ((0, 4), (1, 4))),
        "token_kinds": touch_ends(jax.random.randint(own_keys[1], (TOKEN_COUNT,), 0, RESIDUE_KINDS), jax.random.fold_in(own_keys[1], 1), 0, RESIDUE_KINDS - 1).astype(jnp.int32),
        "first_type_table": normal_values(keys[2], (RESIDUE_KINDS, CZ), 0.5, 3.0),
        "second_type_table": normal_values(keys[3], (RESIDUE_KINDS, CZ), 0.5, 3.0),
        "alignment_state": normal_values(own_keys[4], (ALIGN_ROWS, TOKEN_COUNT * ALIGN_FEATURES), 1.0, 6.0, ((1, 16),)),
        "alignment_index": touch_ends(jax.random.randint(own_keys[5], (ALIGN_ROWS, TOKEN_COUNT), 0, RESIDUE_KINDS), jax.random.fold_in(own_keys[5], 1), 0, RESIDUE_KINDS - 1).astype(jnp.int32),
        "alignment_table": normal_values(keys[6], (RESIDUE_KINDS, ALIGN_FEATURES), 0.5, 3.0),
        "first_weight": normal_values(keys[7], (ALIGN_FEATURES, C), ALIGN_FEATURES ** -0.5, 1.0),
        "second_weight": normal_values(keys[8], (ALIGN_FEATURES, C), ALIGN_FEATURES ** -0.5, 1.0),
        "outer_product_weight": normal_values(keys[9], (C * C, CZ), (C * C // 64) ** -0.5, 1.5),
        "outer_product_bias": normal_values(keys[10], (CZ,), 1.0, 4.0),
        "pair_block_mask": touch_ends((jax.random.randint(own_keys[11], (TOKEN_COUNT // MB, TOKEN_COUNT // MB), 0, 4) < 3).astype(jnp.int32), jax.random.fold_in(own_keys[11], 1), 0, 1),
        "transition_gain": jnp.clip(1.0 + 0.15 * jax.random.normal(keys[12], (CZ,), jnp.float32), 0.25, 1.75),
        "transition_gate_up": normal_values(keys[13], (CZ, 2 * HID), CZ ** -0.5, 0.5),
        "transition_down": normal_values(keys[14], (HID, CZ), HID ** -0.5, 0.25),
        "distance_weight": normal_values(keys[15], (CZ, BINS), CZ ** -0.5, 0.5),
        "distance_bias": normal_values(keys[16], (BINS,), 1.0, 4.0, (), jnp.float32),
    }


EPSILON = 1e-05

def reference(pair_state, token_kinds, first_type_table, second_type_table, alignment_state, alignment_index, alignment_table, first_weight, second_weight, outer_product_weight, outer_product_bias, pair_block_mask, transition_gain, transition_gate_up, transition_down, distance_weight, distance_bias):
    embedded_input = (alignment_state.reshape(ALIGN_ROWS, TOKEN_COUNT, ALIGN_FEATURES).astype(jnp.float32) + alignment_table[alignment_index].astype(jnp.float32)).astype(jnp.bfloat16)
    left_proj = jnp.einsum('snm,mc->snc', embedded_input.astype(jnp.float32), first_weight.astype(jnp.float32)).astype(jnp.bfloat16)
    right_proj = jnp.einsum('snm,mc->snc', embedded_input.astype(jnp.float32), second_weight.astype(jnp.float32)).astype(jnp.bfloat16)
    right_float = right_proj.astype(jnp.float32)
    left_embed = first_type_table[token_kinds].astype(jnp.float32)
    right_embed = second_type_table[token_kinds].astype(jnp.float32)
    mask_full = jnp.repeat(jnp.repeat(pair_block_mask, MB, axis=0), MB, axis=1).astype(jnp.float32)
    block_rows = 16
    dist_float = distance_weight.astype(jnp.float32)

    def one_block(block_index):
        first_row = block_index * block_rows
        left_part = lax.dynamic_slice_in_dim(left_proj, first_row, block_rows, 1).astype(jnp.float32)
        outer_average = jnp.einsum('sic,sje->ijce', left_part, right_float) / ALIGN_ROWS
        outer_average = outer_average.astype(jnp.bfloat16).reshape(block_rows * TOKEN_COUNT, C * C)
        update = jnp.dot(outer_average, outer_product_weight, preferred_element_type=jnp.float32).reshape(block_rows, TOKEN_COUNT, CZ)
        update = update + outer_product_bias.astype(jnp.float32)
        pair_part = lax.dynamic_slice_in_dim(pair_state, first_row, block_rows, 0).astype(jnp.float32)
        embed_part = lax.dynamic_slice_in_dim(left_embed, first_row, block_rows, 0)
        mask_part = lax.dynamic_slice_in_dim(mask_full, first_row, block_rows, 0)
        start_pair = pair_part + embed_part[:, None, :] + right_embed[None, :, :] + mask_part[:, :, None] * update
        chan_mean = lax.optimization_barrier(jnp.mean(start_pair, axis=-1, keepdims=True))
        centered = start_pair - chan_mean
        chan_var = lax.optimization_barrier(jnp.mean(centered * centered, axis=-1, keepdims=True))
        normed = (centered * lax.rsqrt(chan_var + EPSILON) * transition_gain).astype(jnp.bfloat16)
        gate_up = jnp.dot(normed.reshape(block_rows * TOKEN_COUNT, CZ), transition_gate_up, preferred_element_type=jnp.float32)
        hidden = (jax.nn.silu(gate_up[:, :HID]) * gate_up[:, HID:]).astype(jnp.bfloat16)
        result = (start_pair + jnp.dot(hidden, transition_down, preferred_element_type=jnp.float32).reshape(block_rows, TOKEN_COUNT, CZ)).astype(jnp.bfloat16)
        part = jnp.einsum('ijc,cb->ijb', result.astype(jnp.float32), dist_float).astype(jnp.bfloat16)
        return (result, part)
    pair_out, dist_part = lax.map(one_block, jnp.arange(TOKEN_COUNT // block_rows, dtype=jnp.int32))
    pair_out = pair_out.reshape(TOKEN_COUNT, TOKEN_COUNT, CZ)
    dist_part = dist_part.reshape(TOKEN_COUNT, TOKEN_COUNT, BINS)

    def dist_block(block_index):
        first_row = block_index * block_rows
        direct = lax.dynamic_slice_in_dim(dist_part, first_row, block_rows, 0).astype(jnp.float32)
        mirrored = jnp.swapaxes(lax.dynamic_slice_in_dim(dist_part, first_row, block_rows, 1), 0, 1).astype(jnp.float32)
        return (direct + mirrored + distance_bias).astype(jnp.bfloat16)
    distogram = lax.map(dist_block, jnp.arange(TOKEN_COUNT // block_rows, dtype=jnp.int32)).reshape(TOKEN_COUNT, TOKEN_COUNT * BINS)
    return (pair_out, distogram)
```

```python
import functools

import jax
import jax.numpy as jnp
from jax import lax
from jax.experimental import pallas as pl
from jax.experimental.pallas import tpu as pltpu
from jax.sharding import PartitionSpec as P

EPSILON = 1e-05
F32 = jnp.float32
BF16 = jnp.bfloat16
NT = (((1,), (1,)), ((), ()))
TN = (((0,), (0,)), ((), ()))
VMEM_BYTES = 48 * 1024 * 1024


def iota(shape, dim):
    return lax.broadcasted_iota(jnp.int32, shape, dim)


def dot(a, b):
    return jnp.dot(a, b, preferred_element_type=F32)


def spread(rows, row_key, weight, columns, column_key, keep):
    left = (row_key(iota((rows, weight.shape[0]), 0)) == iota((rows, weight.shape[0]), 1)).astype(BF16)
    right = (column_key(iota((weight.shape[1], columns), 1)) == iota((weight.shape[1], columns), 0)).astype(BF16)
    full = dot(dot(left, weight).astype(BF16), right)
    at = iota((rows, columns), 0), iota((rows, columns), 1)
    return jnp.where(keep(*at), full, 0.0).astype(BF16)


def embed_kernel(state_ref, index_ref, table_ref, out_ref):
    depth, width = state_ref.shape
    tokens = index_ref.shape[1]
    kinds, features = table_ref.shape
    spread_tokens = (iota((tokens, tokens * kinds), 1) // kinds == iota((tokens, tokens * kinds), 0)).astype(BF16)
    wide = dot(index_ref[...].astype(F32).astype(BF16), spread_tokens)
    onehot = (wide == (iota(wide.shape, 1) % kinds).astype(F32)).astype(BF16)
    group = min(tokens, 256 // features)
    table = spread(
        group * kinds,
        lambda r: r % kinds,
        table_ref[...],
        group * features,
        lambda c: c % features,
        lambda r, c: r // kinds == c // features,
    )
    for start in range(0, tokens, group):
        at = slice(start * features, (start + group) * features)
        rows = dot(onehot[:, start * kinds : (start + group) * kinds], table)
        out_ref[:, at] = (state_ref[:, at].astype(F32) + rows).astype(BF16)


def weights_kernel(
    row_ref,
    kinds_ref,
    first_ref,
    second_ref,
    outer_ref,
    distance_ref,
    first_out,
    second_out,
    outer_out,
    distance_out,
    wide,
    rows,
):
    channels = outer_ref.shape[1]
    length = first_out.shape[0]
    side = wide.shape[0] // 32
    kinds = kinds_ref[...]
    onehot = (iota((first_ref.shape[0], kinds.shape[1]), 0) == kinds).astype(BF16)
    for which, (table, out) in enumerate(((first_ref, first_out), (second_ref, second_out))):
        rows[...] = lax.dot_general(onehot, table[...], TN, preferred_element_type=F32)
        out[...] = rows[pl.ds(pl.multiple_of(row_ref[which] * length, length), length), :]
    wide[...] = outer_ref[...].astype(F32)
    zero = jnp.zeros((side, channels), BF16)
    for e in range(32):
        part = wide[pl.ds(e, side, stride=32), :].astype(BF16)
        outer_out[pl.ds(2 * e * side, side), :] = jnp.concatenate([part, zero], axis=1)
        outer_out[pl.ds((2 * e + 1) * side, side), :] = jnp.concatenate([zero, part], axis=1)
    weight = distance_ref[...]
    none = jnp.zeros_like(weight)
    distance_out[...] = jnp.concatenate(
        [jnp.concatenate([weight, none], axis=1), jnp.concatenate([none, weight], axis=1)], axis=0
    )


def project_kernel(blocks, *refs):
    place_ref = refs[0]
    lefts, rights = refs[1 : 1 + blocks], refs[1 + blocks : 1 + 2 * blocks]
    first_ref, second_ref, left_out, right_out, left_all, right_all = refs[1 + 2 * blocks :]
    width = lefts[0].shape[1]
    depth = lefts[0].shape[0]
    features, c_width = first_ref.shape
    for which, (parts, whole) in enumerate(((lefts, left_all), (rights, right_all))):
        for k, part in enumerate(parts):
            block = lax.rem(place_ref[which] + k, blocks)
            whole[:, pl.ds(pl.multiple_of(block * width, width), width)] = part[...]
    tokens = blocks * width // features
    lanes = 2 * 2 * c_width
    weight = spread(
        8 * features,
        lambda r: r % features,
        first_ref[...],
        4 * lanes,
        lambda c: c % c_width,
        lambda r, c: r // features == 2 * (c // lanes) + c % (lanes // 2) // c_width,
    )
    half = iota((depth, 4 * lanes), 1) % lanes < lanes // 2
    for t in range(tokens // 8):
        both = dot(left_all[:, t * 8 * features : (t + 1) * 8 * features], weight)
        at = slice(t * 4 * lanes, (t + 1) * 4 * lanes)
        left_out[0:depth, at] = jnp.where(half, both, 0.0).astype(BF16)
        left_out[depth : 2 * depth, at] = jnp.where(half, 0.0, both).astype(BF16)
    e_width = second_ref.shape[1]
    turned = lax.dot_general(
        (iota((8 * e_width, e_width), 0) // 8 == iota((8 * e_width, e_width), 1)).astype(BF16),
        second_ref[...],
        NT,
        preferred_element_type=F32,
    ).astype(BF16)
    repeat = (iota((features, 8 * features), 1) % features == iota((features, 8 * features), 0)).astype(BF16)
    shape = (8 * e_width, 8 * features)
    weight = jnp.where(
        iota(shape, 0) % 8 == iota(shape, 1) // features, dot(turned, repeat), 0.0
    ).astype(BF16)
    low = iota((8, 2 * depth), 1) < depth
    for t in range(0, tokens // 8, 2):
        sides = []
        for u in (t, t + 1):
            part = right_all[:, u * 8 * features : (u + 1) * 8 * features]
            twice = jnp.concatenate([part, part], axis=0)
            sides.append(lax.dot_general(weight, twice, NT, preferred_element_type=F32))
        for g in range(e_width // 2):
            rows = [
                jnp.where(low, s[16 * g : 16 * g + 8], s[16 * g + 8 : 16 * g + 16]) for s in sides
            ]
            right_out[pl.ds(g * tokens + t * 8, 16), :] = jnp.concatenate(rows, axis=0).astype(BF16)


def pair_kernel(
    first_block,
    mask_ref,
    left_ref,
    right_ref,
    pair_ref,
    first_ref,
    second_ref,
    bias_ref,
    gain_ref,
    outer_ref,
    gate_up_ref,
    down_ref,
    distance_ref,
    *rest,
):
    pair_out, dist_out, outer, start = rest[-4:]
    rows, length, channels = pair_ref.shape
    pairs = rows // 2
    depth = right_ref.shape[1] // 2
    lanes = right_ref.shape[1]
    groups = right_ref.shape[0] // length
    hid = down_ref.shape[0]
    block = pl.program_id(0) + first_block
    for p in range(0, pairs, 2):
        weight = left_ref[:, p * lanes : (p + 2) * lanes]
        for g in range(0, groups, 4):
            got = dot(right_ref[g * length : (g + 4) * length, :], weight).astype(BF16)
            for q in range(2):
                for h in range(4):
                    outer[(p + q) * length : (p + q + 1) * length, (g + h) * lanes : (g + h + 1) * lanes] = got[
                        h * length : (h + 1) * length, q * lanes : (q + 1) * lanes
                    ]
    update = dot(outer[...], outer_ref[...])
    mask_columns = mask_ref.shape[1]
    mask = jnp.concatenate(
        [
            jnp.full((length // mask_columns, channels), mask_ref[block, m].astype(F32), F32)
            for m in range(mask_columns)
        ],
        axis=0,
    )
    bias = second_ref[...] + mask * bias_ref[...].astype(F32)
    mask = mask * (1.0 / depth)
    normed = []
    for p in range(pairs):
        for q in range(2):
            i = 2 * p + q
            value = (
                pair_ref[i].astype(F32)
                + (first_ref[i : i + 1, :] + bias)
                + mask * update[p * length : (p + 1) * length, q * channels : (q + 1) * channels]
            )
            start[q, p * length : (p + 1) * length, :] = value
    for q in range(2):
        value = start[q]
        mean = jnp.mean(value, axis=-1, keepdims=True)
        centered = value - mean
        variance = jnp.mean(centered * centered, axis=-1, keepdims=True)
        normed = (centered * lax.rsqrt(variance + EPSILON) * gain_ref[...]).astype(BF16)
        for n in range(0, hid, 256):
            gate = dot(normed, gate_up_ref[:, n : n + 256])
            up = dot(normed, gate_up_ref[:, hid + n : hid + n + 256])
            hidden = (0.5 * gate * (1.0 + jnp.tanh(0.5 * gate)) * up).astype(BF16)
            value = value + dot(hidden, down_ref[n : n + 256, :])
        start[q] = value
    result = [start[q].astype(BF16) for q in range(2)]
    for p in range(pairs):
        for q in range(2):
            pair_out[2 * p + q] = result[q][p * length : (p + 1) * length]
    dist = dot(jnp.concatenate(result, axis=1), distance_ref[...]).astype(BF16)
    width = dist.shape[1]
    for p in range(pairs):
        dist_out[:, p * width : (p + 1) * width] = dist[p * length : (p + 1) * length]


def final_kernel(own_ref, mirror_ref, bias_ref, out_ref):
    out_ref[...] = (own_ref[...].astype(F32) + mirror_ref[...].astype(F32) + bias_ref[...]).astype(BF16)


def params():
    return pltpu.CompilerParams(vmem_limit_bytes=VMEM_BYTES)


VMEM = pl.BlockSpec(memory_space=pltpu.VMEM)
SMEM = pl.BlockSpec(memory_space=pltpu.SMEM)


def local(
    row_count,
    col_count,
    pair_state,
    token_kinds,
    first_type_table,
    second_type_table,
    alignment_state,
    alignment_index,
    alignment_table,
    first_weight,
    second_weight,
    outer_product_weight,
    outer_product_bias,
    pair_block_mask,
    transition_gain,
    transition_gate_up,
    transition_down,
    distance_weight,
    distance_bias,
):
    length = pair_state.shape[0]
    channels = pair_state.shape[2]
    depth = alignment_index.shape[0]
    c_width, e_width = first_weight.shape[1], second_weight.shape[1]
    bins = distance_weight.shape[1]
    axes = ("row", "col")
    place = jnp.stack([lax.axis_index("col"), lax.axis_index("row")]).astype(jnp.int32)

    embedded = pl.pallas_call(
        embed_kernel,
        out_shape=jax.ShapeDtypeStruct(alignment_state.shape, BF16),
        in_specs=[VMEM] * 3,
        out_specs=VMEM,
        compiler_params=params(),
        name="embed",
    )(alignment_state, alignment_index, alignment_table)

    def moved(value, target):
        pairs = [
            (r * col_count + c, target(r, c)[0] * col_count + target(r, c)[1])
            for r in range(row_count)
            for c in range(col_count)
        ]
        return lax.ppermute(value, axes, pairs)

    rights = [
        moved(embedded, lambda r, c, k=k: ((c - k) % row_count, r)) for k in range(col_count)
    ]
    lefts = [embedded] + [
        moved(embedded, lambda r, c, k=k: (r, (c - k) % col_count)) for k in range(1, col_count)
    ]

    first_rows, second_rows, outer_weight, pair_distance = pl.pallas_call(
        weights_kernel,
        out_shape=(
            jax.ShapeDtypeStruct((length, channels), F32),
            jax.ShapeDtypeStruct((length, channels), F32),
            jax.ShapeDtypeStruct((2 * c_width * e_width, 2 * channels), BF16),
            jax.ShapeDtypeStruct((2 * channels, 2 * bins), BF16),
        ),
        in_specs=[SMEM] + [VMEM] * 5,
        out_specs=(VMEM,) * 4,
        scratch_shapes=[
            pltpu.VMEM(outer_product_weight.shape, F32),
            pltpu.VMEM((token_kinds.shape[0], channels), F32),
        ],
        compiler_params=params(),
        name="weights",
    )(
        place[::-1],
        token_kinds.reshape(1, -1),
        first_type_table,
        second_type_table,
        outer_product_weight,
        distance_weight,
    )

    left_tiles, right_tiles = pl.pallas_call(
        functools.partial(project_kernel, col_count),
        out_shape=(
            jax.ShapeDtypeStruct((2 * depth, 2 * length * c_width), BF16),
            jax.ShapeDtypeStruct((e_width // 2 * length, 2 * depth), BF16),
        ),
        in_specs=[SMEM] + [VMEM] * (2 * col_count + 2),
        out_specs=(VMEM,) * 2,
        scratch_shapes=[pltpu.VMEM((depth, col_count * alignment_state.shape[1]), BF16)] * 2,
        compiler_params=params(),
        name="project",
    )(place, *lefts, *rights, first_weight, second_weight)

    blocks = pair_block_mask.shape[0]
    rows = length // blocks
    fixed = lambda shape: pl.BlockSpec(shape, lambda b: (0,) * len(shape))
    pair_out, dist = pl.pallas_call(
        functools.partial(pair_kernel, 0),
        grid=(blocks,),
        out_shape=(
            jax.ShapeDtypeStruct(pair_state.shape, BF16),
            jax.ShapeDtypeStruct((length, length * bins), BF16),
        ),
        in_specs=[
            SMEM,
            pl.BlockSpec((2 * depth, 2 * rows * c_width), lambda b: (0, b)),
            fixed(right_tiles.shape),
            pl.BlockSpec((rows, length, channels), lambda b: (b, 0, 0)),
            pl.BlockSpec((rows, channels), lambda b: (b, 0)),
            fixed(second_rows.shape),
            fixed((1, channels)),
            fixed((1, channels)),
            fixed(outer_weight.shape),
            fixed(transition_gate_up.shape),
            fixed(transition_down.shape),
            fixed(pair_distance.shape),
        ],
        out_specs=(
            pl.BlockSpec((rows, length, channels), lambda b: (b, 0, 0)),
            pl.BlockSpec((length, rows * bins), lambda b: (0, b)),
        ),
        scratch_shapes=[
            pltpu.VMEM((rows // 2 * length, 2 * c_width * e_width), BF16),
            pltpu.VMEM((2, rows // 2 * length, channels), F32),
        ],
        compiler_params=params(),
        name="pairs",
    )(
        pair_block_mask,
        left_tiles,
        right_tiles,
        pair_state,
        first_rows,
        second_rows,
        outer_product_bias.reshape(1, -1),
        transition_gain.reshape(1, -1),
        outer_weight,
        transition_gate_up,
        transition_down,
        pair_distance,
    )
    mirror = moved(dist, lambda r, c: (c, r))
    own = dist.reshape(length, length, bins).transpose(1, 0, 2).reshape(length, length * bins)
    distogram = pl.pallas_call(
        final_kernel,
        out_shape=jax.ShapeDtypeStruct((length, length * bins), BF16),
        in_specs=[VMEM] * 3,
        out_specs=VMEM,
        compiler_params=params(),
        name="final",
    )(own, mirror, jnp.tile(distance_bias, length).reshape(1, -1))
    return pair_out, distogram


def solution(mesh):
    split = P(("conf", "row"), "col")
    tokens = P(None, ("conf", "row", "col"))
    in_specs = (
        P(("conf", "row"), "col", None),
        P("conf"),
        P(),
        P(),
        tokens,
        tokens,
        P(),
        P(),
        P(),
        P(),
        P(),
        split,
        P(),
        P(),
        P(),
        P(),
        P(),
    )
    return jax.shard_map(
        functools.partial(local, mesh.shape["row"], mesh.shape["col"]),
        mesh=mesh,
        in_specs=in_specs,
        out_specs=(P(("conf", "row"), "col", None), split),
        check_vma=False,
    )
```

```python
import functools

import jax
import jax.numpy as jnp
from jax import lax
from jax.experimental import pallas as pl
from jax.experimental.pallas import tpu as pltpu
from jax.sharding import PartitionSpec as P

EPSILON = 1e-05
F32 = jnp.float32
BF16 = jnp.bfloat16
NT = (((1,), (1,)), ((), ()))
TN = (((0,), (0,)), ((), ()))
MIB = 1024 * 1024


def iota(shape, dim):
    return lax.broadcasted_iota(jnp.int32, shape, dim)


def dot(a, b):
    return jnp.dot(a, b, preferred_element_type=F32)


def spread(rows, row_key, weight, columns, column_key, keep):
    left = (row_key(iota((rows, weight.shape[0]), 0)) == iota((rows, weight.shape[0]), 1)).astype(BF16)
    right = (column_key(iota((weight.shape[1], columns), 1)) == iota((weight.shape[1], columns), 0)).astype(BF16)
    full = dot(dot(left, weight).astype(BF16), right)
    at = iota((rows, columns), 0), iota((rows, columns), 1)
    return jnp.where(keep(*at), full, 0.0).astype(BF16)


def fetch(sources, targets, sems):
    copies = [pltpu.make_async_copy(s, t, sems.at[n]) for n, (s, t) in enumerate(zip(sources, targets, strict=True))]
    for copy in copies:
        copy.start()
    return copies


def embed_kernel(state_hbm, index_hbm, table_hbm, out_ref, state_ref, index_ref, table_ref, sems):
    copies = fetch((index_hbm, table_hbm, state_hbm), (index_ref, table_ref, state_ref), sems)
    tokens = index_ref.shape[0]
    kinds, features = table_ref.shape
    group = min(tokens, 256 // features)
    copies[1].wait()
    table = spread(
        group * kinds,
        lambda r: r % kinds,
        table_ref[...],
        group * features,
        lambda c: c % features,
        lambda r, c: r // kinds == c // features,
    )
    spread_tokens = (iota((tokens, tokens * kinds), 1) // kinds == iota((tokens, tokens * kinds), 0)).astype(BF16)
    copies[0].wait()
    wide = lax.dot_general(
        index_ref[...].astype(F32).astype(BF16), spread_tokens, TN, preferred_element_type=F32
    )
    onehot = (wide == (iota(wide.shape, 1) % kinds).astype(F32)).astype(BF16)
    copies[2].wait()
    for start in range(0, tokens, group):
        at = slice(start * features, (start + group) * features)
        rows = dot(onehot[:, start * kinds : (start + group) * kinds], table)
        out_ref[:, at] = (state_ref[:, at].astype(F32) + rows).astype(BF16)


def weights_kernel(
    place_ref,
    kinds_hbm,
    first_hbm,
    second_hbm,
    outer_hbm,
    bias_hbm,
    mask_hbm,
    pair_hbm,
    gate_up_hbm,
    down_hbm,
    left_hbm,
    right_hbm,
    gain_hbm,
    distance_hbm,
    last_hbm,
    first_out,
    mask_out,
    base_out,
    outer_out,
    pair_out,
    gate_up_out,
    down_out,
    gain_out,
    left_out,
    right_out,
    distance_out,
    last_out,
    kinds_ref,
    first_ref,
    second_ref,
    outer_ref,
    bias_ref,
    mask_ref,
    left_ref,
    right_ref,
    distance_ref,
    last_ref,
    wide,
    rows,
    sems,
):
    copies = fetch(
        (left_hbm, right_hbm, kinds_hbm, first_hbm, second_hbm, bias_hbm, mask_hbm, distance_hbm, last_hbm)
        + (outer_hbm, pair_hbm, gate_up_hbm, down_hbm, gain_hbm),
        (left_ref, right_ref, kinds_ref, first_ref, second_ref, bias_ref, mask_ref, distance_ref, last_ref)
        + (outer_ref, pair_out, gate_up_out, down_out, gain_out),
        sems,
    )
    channels = outer_ref.shape[1]
    length = first_out.shape[0]
    side = left_hbm.shape[1]
    steps = outer_ref.shape[0] // side
    for copy in copies[:9]:
        copy.wait()
    features, c_width = left_ref.shape
    lanes = 4 * c_width
    left_out[...] = spread(
        8 * features,
        lambda r: r % features,
        left_ref[...],
        4 * lanes,
        lambda c: c % c_width,
        lambda r, c: r // features == 2 * (c // lanes) + c % (lanes // 2) // c_width,
    )
    e_width = right_ref.shape[1]
    turned = lax.dot_general(
        (iota((8 * e_width, e_width), 0) // 8 == iota((8 * e_width, e_width), 1)).astype(BF16),
        right_ref[...],
        NT,
        preferred_element_type=F32,
    ).astype(BF16)
    repeat = (iota((features, 8 * features), 1) % features == iota((features, 8 * features), 0)).astype(BF16)
    shape = right_out.shape
    right_out[...] = jnp.where(
        iota(shape, 0) % 8 == iota(shape, 1) // features, dot(turned, repeat), 0.0
    ).astype(BF16)
    weight = distance_ref[...]
    none = jnp.zeros_like(weight)
    distance_out[...] = jnp.concatenate(
        [jnp.concatenate([weight, none], axis=1), jnp.concatenate([none, weight], axis=1)], axis=0
    )
    last_out[...] = jnp.concatenate([last_ref[...], last_ref[...]], axis=1)
    kinds = kinds_ref[...]
    onehot = (iota((first_ref.shape[0], kinds.shape[1]), 0) == kinds).astype(BF16)
    rows[...] = lax.dot_general(onehot, first_ref[...], TN, preferred_element_type=F32)
    first_out[...] = rows[pl.ds(pl.multiple_of(place_ref[1] * length, length), length), :]
    rows[...] = lax.dot_general(onehot, second_ref[...], TN, preferred_element_type=F32)
    second = rows[pl.ds(pl.multiple_of(place_ref[0] * length, length), length), :]
    blocks, columns = mask_ref.shape
    reach = (iota((length, columns), 0) // (length // columns) == iota((length, columns), 1)).astype(BF16)
    mask = lax.dot_general(
        reach, mask_ref[...].astype(F32).astype(BF16), NT, preferred_element_type=F32
    )
    bias = bias_ref[...].astype(F32)
    for b in range(blocks):
        part = jnp.broadcast_to(mask[:, b : b + 1], (length, channels))
        mask_out[b] = part
        base_out[b] = second + part * bias
    copies[9].wait()
    wide[...] = outer_ref[...].astype(F32)
    zero = jnp.zeros((side, channels), BF16)
    for e in range(steps):
        part = wide[pl.ds(e, side, stride=steps), :].astype(BF16)
        outer_out[pl.ds(2 * e * side, side), :] = jnp.concatenate([part, zero], axis=1)
        outer_out[pl.ds((2 * e + 1) * side, side), :] = jnp.concatenate([zero, part], axis=1)
    for copy in copies[10:]:
        copy.wait()


def project_kernel(blocks, features, *refs):
    place_ref = refs[0]
    lefts, rights = refs[1 : 1 + blocks], refs[1 + blocks : 1 + 2 * blocks]
    first_ref, second_ref, left_out, right_out, left_all, right_all = refs[1 + 2 * blocks :]
    depth, width = lefts[0].shape
    for which, (parts, whole) in enumerate(((lefts, left_all), (rights, right_all))):
        for k, part in enumerate(parts):
            block = lax.rem(place_ref[which] + k, blocks)
            whole[:, pl.ds(pl.multiple_of(block * width, width), width)] = part[...]
    tokens = blocks * width // features
    group, columns = first_ref.shape
    half = iota((depth, columns), 1) % (columns // 4) < columns // 8
    for t in range(tokens // 8):
        both = dot(left_all[:, t * group : (t + 1) * group], first_ref[...])
        at = slice(t * columns, (t + 1) * columns)
        left_out[0:depth, at] = jnp.where(half, both, 0.0).astype(BF16)
        left_out[depth : 2 * depth, at] = jnp.where(half, 0.0, both).astype(BF16)
    low = iota((8, 2 * depth), 1) < depth
    for t in range(0, tokens // 8, 2):
        sides = []
        for u in (t, t + 1):
            part = right_all[:, u * group : (u + 1) * group]
            twice = jnp.concatenate([part, part], axis=0)
            sides.append(lax.dot_general(second_ref[...], twice, NT, preferred_element_type=F32))
        for g in range(second_ref.shape[0] // 16):
            rows = [
                jnp.where(low, s[16 * g : 16 * g + 8], s[16 * g + 8 : 16 * g + 16]) for s in sides
            ]
            right_out[pl.ds(g * tokens + t * 8, 16), :] = jnp.concatenate(rows, axis=0).astype(BF16)


def pair_kernel(
    block,
    left_ref,
    right_ref,
    pair_ref,
    first_ref,
    mask_ref,
    base_ref,
    gain_ref,
    outer_ref,
    gate_up_ref,
    down_ref,
    distance_ref,
    *rest,
):
    pair_out, dist_out, outer, start = rest[-4:]
    rows, length, channels = pair_out.shape
    first_row = block * rows
    pairs = rows // 2
    depth = right_ref.shape[1] // 2
    lanes = right_ref.shape[1]
    groups = right_ref.shape[0] // length
    hid = down_ref.shape[0]
    bins = distance_ref.shape[0] // 2
    for p in range(0, pairs, 2):
        tile = block * pairs + p
        weight = left_ref[:, tile * lanes : (tile + 2) * lanes]
        for g in range(0, groups, 4):
            got = dot(right_ref[g * length : (g + 4) * length, :], weight).astype(BF16)
            for q in range(2):
                for h in range(4):
                    outer[(p + q) * length : (p + q + 1) * length, (g + h) * lanes : (g + h + 1) * lanes] = got[
                        h * length : (h + 1) * length, q * lanes : (q + 1) * lanes
                    ]
    update = dot(outer[...], outer_ref[...])
    mask = mask_ref[block] * (1.0 / depth)
    base = base_ref[block]
    for p in range(pairs):
        for q in range(2):
            i = first_row + 2 * p + q
            value = (
                pair_ref[i].astype(F32)
                + (first_ref[i : i + 1, :] + base)
                + mask * update[p * length : (p + 1) * length, q * channels : (q + 1) * channels]
            )
            start[q, p * length : (p + 1) * length, :] = value
    for q in range(2):
        value = start[q]
        mean = jnp.mean(value, axis=-1, keepdims=True)
        centered = value - mean
        variance = jnp.mean(centered * centered, axis=-1, keepdims=True)
        normed = (centered * lax.rsqrt(variance + EPSILON) * gain_ref[...]).astype(BF16)
        for n in range(0, hid, 256):
            gate = dot(normed, gate_up_ref[:, n : n + 256])
            up = dot(normed, gate_up_ref[:, hid + n : hid + n + 256])
            hidden = (0.5 * gate * (1.0 + jnp.tanh(0.5 * gate)) * up).astype(BF16)
            value = value + dot(hidden, down_ref[n : n + 256, :])
        start[q] = value
    result = [start[q].astype(BF16) for q in range(2)]
    for p in range(pairs):
        for q in range(2):
            pair_out[2 * p + q] = result[q][p * length : (p + 1) * length]
    dist = lax.dot_general(
        jnp.concatenate(result, axis=1), distance_ref[...], NT, preferred_element_type=F32
    ).astype(BF16)
    for p in range(pairs):
        dist_out[:, 2 * p * bins : 2 * (p + 1) * bins] = dist[p * length : (p + 1) * length]


def own_kernel(blocks, *refs):
    parts, dists = refs[:blocks], refs[blocks : 2 * blocks]
    pair_out, own_ref, sems = refs[2 * blocks :]
    rows = parts[0].shape[0]
    copies = fetch(parts, [pair_out.at[pl.ds(n * rows, rows)] for n in range(blocks)], sems)
    pairs = rows // 2
    lanes = dists[0].shape[1] // pairs
    low = iota((pairs, lanes), 1) < lanes // 2
    for n, dist in enumerate(dists):
        tiles = jnp.stack([dist[:, p * lanes : (p + 1) * lanes].astype(F32) for p in range(pairs)])
        turned = jnp.swapaxes(tiles, 0, 1)
        for j in range(0, turned.shape[0], 2):
            first, second = turned[j], turned[j + 1]
            own_ref[j // 2, pl.ds(n * rows, pairs, stride=2), :] = jnp.where(
                low, first, pltpu.roll(second, lanes // 2, 1)
            )
            own_ref[j // 2, pl.ds(n * rows + 1, pairs, stride=2), :] = jnp.where(
                low, pltpu.roll(first, lanes // 2, 1), second
            )
    for copy in copies:
        copy.wait()


def final_kernel(blocks, own_ref, bias_ref, *refs):
    out_ref = refs[blocks]
    for n in range(blocks):
        width = refs[n].shape[1]
        lanes = bias_ref.shape[1]
        for t in range(0, width, lanes):
            at = slice(n * width + t, n * width + t + lanes)
            value = own_ref[at.start // lanes] + refs[n][:, t : t + lanes].astype(F32) + bias_ref[...]
            out_ref[:, at] = value.astype(BF16)


COST = pl.CostEstimate(flops=0, bytes_accessed=0, transcendentals=0)


def params(mib):
    return pltpu.CompilerParams(vmem_limit_bytes=mib * MIB)


def in_hbm(*arrays):
    return [pltpu.with_memory_space_constraint(a, pltpu.HBM) for a in arrays]


VMEM = pl.BlockSpec(memory_space=pltpu.VMEM)
SMEM = pl.BlockSpec(memory_space=pltpu.SMEM)
HBM = pl.BlockSpec(memory_space=pltpu.HBM)


def local(
    row_count,
    col_count,
    pair_state,
    token_kinds,
    first_type_table,
    second_type_table,
    alignment_state,
    alignment_index,
    alignment_table,
    first_weight,
    second_weight,
    outer_product_weight,
    outer_product_bias,
    pair_block_mask,
    transition_gain,
    transition_gate_up,
    transition_down,
    distance_weight,
    distance_bias,
):
    length = pair_state.shape[0]
    channels = pair_state.shape[2]
    depth = alignment_index.shape[0]
    features, c_width = first_weight.shape
    e_width = second_weight.shape[1]
    bins = distance_weight.shape[1]
    axes = ("row", "col")
    place = jnp.stack([lax.axis_index("col"), lax.axis_index("row")]).astype(jnp.int32)

    turned_index = alignment_index.T
    embedded = pl.pallas_call(
        embed_kernel,
        out_shape=jax.ShapeDtypeStruct(alignment_state.shape, BF16),
        in_specs=[HBM] * 3,
        out_specs=VMEM,
        scratch_shapes=[
            pltpu.VMEM(alignment_state.shape, BF16),
            pltpu.VMEM(turned_index.shape, jnp.int32),
            pltpu.VMEM(alignment_table.shape, BF16),
            pltpu.SemaphoreType.DMA((3,)),
        ],
        compiler_params=params(4),
        cost_estimate=COST,
        name="embed",
    )(*in_hbm(alignment_state, turned_index, alignment_table))

    def moved(value, target):
        pairs = [
            (r * col_count + c, target(r, c)[0] * col_count + target(r, c)[1])
            for r in range(row_count)
            for c in range(col_count)
        ]
        return lax.ppermute(value, axes, pairs)

    rights = [
        moved(embedded, lambda r, c, k=k: ((c - k) % row_count, r)) for k in range(col_count)
    ]
    lefts = [embedded] + [
        moved(embedded, lambda r, c, k=k: (r, (c - k) % col_count)) for k in range(1, col_count)
    ]

    blocks = pair_block_mask.shape[0]
    rows = length // blocks
    maps = jax.ShapeDtypeStruct((blocks, length, channels), F32)
    first_rows, masks, bases, outer_weight, pair_in, gate_up, down, gain, left_weight, right_weight, turned_distance, last = pl.pallas_call(
        weights_kernel,
        out_shape=(
            jax.ShapeDtypeStruct((length, channels), F32),
            maps,
            maps,
            jax.ShapeDtypeStruct((2 * c_width * e_width, 2 * channels), BF16),
            jax.ShapeDtypeStruct(pair_state.shape, BF16),
            jax.ShapeDtypeStruct(transition_gate_up.shape, BF16),
            jax.ShapeDtypeStruct(transition_down.shape, BF16),
            jax.ShapeDtypeStruct((1, channels), F32),
            jax.ShapeDtypeStruct((8 * features, 16 * c_width), BF16),
            jax.ShapeDtypeStruct((8 * e_width, 8 * features), BF16),
            jax.ShapeDtypeStruct((2 * bins, 2 * channels), BF16),
            jax.ShapeDtypeStruct((1, 2 * bins), F32),
        ),
        in_specs=[SMEM] + [HBM] * 14,
        out_specs=(VMEM,) * 12,
        scratch_shapes=[
            pltpu.VMEM((1, token_kinds.shape[0]), jnp.int32),
            pltpu.VMEM(first_type_table.shape, BF16),
            pltpu.VMEM(second_type_table.shape, BF16),
            pltpu.VMEM(outer_product_weight.shape, BF16),
            pltpu.VMEM((1, channels), BF16),
            pltpu.VMEM(pair_block_mask.shape, jnp.int32),
            pltpu.VMEM(first_weight.shape, BF16),
            pltpu.VMEM(second_weight.shape, BF16),
            pltpu.VMEM((bins, channels), BF16),
            pltpu.VMEM((1, bins), F32),
            pltpu.VMEM(outer_product_weight.shape, F32),
            pltpu.VMEM((token_kinds.shape[0], channels), F32),
            pltpu.SemaphoreType.DMA((14,)),
        ],
        compiler_params=params(8),
        cost_estimate=COST,
        name="weights",
    )(
        place,
        *in_hbm(
            token_kinds.reshape(1, -1),
            first_type_table,
            second_type_table,
            outer_product_weight,
            outer_product_bias.reshape(1, -1),
            pair_block_mask,
            pair_state,
            transition_gate_up,
            transition_down,
            first_weight,
            second_weight,
            transition_gain.reshape(1, -1),
            distance_weight.T,
            distance_bias.reshape(1, -1),
        ),
    )

    left_tiles, right_tiles = pl.pallas_call(
        functools.partial(project_kernel, col_count, features),
        out_shape=(
            jax.ShapeDtypeStruct((2 * depth, 2 * length * c_width), BF16),
            jax.ShapeDtypeStruct((e_width // 2 * length, 2 * depth), BF16),
        ),
        in_specs=[SMEM] + [VMEM] * (2 * col_count + 2),
        out_specs=(VMEM,) * 2,
        scratch_shapes=[pltpu.VMEM((depth, col_count * alignment_state.shape[1]), BF16)] * 2,
        compiler_params=params(8),
        cost_estimate=COST,
        name="project",
    )(place, *lefts, *rights, left_weight, right_weight)

    pair_parts, dist_parts, mirror_parts = [], [], []
    crossed = None
    for block in range(blocks):
        before = dist_parts[-1:]
        if block % 2 == 0 and crossed is not None:
            before = before + [crossed]
        pair_part, dist_part = pl.pallas_call(
            functools.partial(pair_kernel, block),
            out_shape=(
                jax.ShapeDtypeStruct((rows, length, channels), BF16),
                jax.ShapeDtypeStruct((length, rows * bins), BF16),
            ),
            in_specs=[VMEM] * 11 + [pl.BlockSpec(memory_space=pl.ANY)] * len(before),
            out_specs=(VMEM,) * 2,
            scratch_shapes=[
                pltpu.VMEM((rows // 2 * length, 2 * c_width * e_width), BF16),
                pltpu.VMEM((2, rows // 2 * length, channels), F32),
            ],
            compiler_params=params(16),
            cost_estimate=COST,
            name="pairs",
        )(
            left_tiles,
            right_tiles,
            pair_in,
            first_rows,
            masks,
            bases,
            gain,
            outer_weight,
            gate_up,
            down,
            turned_distance,
            *before,
        )
        pair_parts.append(pair_part)
        dist_parts.append(dist_part)
        if block % 2 == 0:
            crossed = moved(dist_part, lambda r, c: (r, (c + col_count // 2) % col_count))
            mirror_parts.append(moved(crossed, lambda r, c: ((c + col_count // 2) % col_count, r)))
        else:
            mirror_parts.append(moved(dist_part, lambda r, c: (c, r)))
    pair_out, own = pl.pallas_call(
        functools.partial(own_kernel, blocks),
        out_shape=(
            jax.ShapeDtypeStruct(pair_state.shape, BF16),
            jax.ShapeDtypeStruct((length // 2, length, 2 * bins), F32),
        ),
        in_specs=[VMEM] * (2 * blocks),
        out_specs=(HBM, VMEM),
        scratch_shapes=[pltpu.SemaphoreType.DMA((blocks,))],
        compiler_params=params(8),
        cost_estimate=COST,
        name="own",
    )(*pair_parts, *dist_parts)
    distogram = pl.pallas_call(
        functools.partial(final_kernel, blocks),
        out_shape=jax.ShapeDtypeStruct((length, length * bins), BF16),
        in_specs=[VMEM] * (blocks + 2),
        out_specs=VMEM,
        compiler_params=params(8),
        cost_estimate=COST,
        name="final",
    )(own, last, *mirror_parts)
    return pair_out, distogram


def solution(mesh):
    split = P(("conf", "row"), "col")
    tokens = P(None, ("conf", "row", "col"))
    in_specs = (
        P(("conf", "row"), "col", None),
        P("conf"),
        P(),
        P(),
        tokens,
        tokens,
        P(),
        P(),
        P(),
        P(),
        P(),
        split,
        P(),
        P(),
        P(),
        P(),
        P(),
    )
    return jax.shard_map(
        functools.partial(local, mesh.shape["row"], mesh.shape["col"]),
        mesh=mesh,
        in_specs=in_specs,
        out_specs=(P(("conf", "row"), "col", None), split),
        check_vma=False,
    )
```

```python
import functools

import jax
import jax.numpy as jnp
from jax import lax
from jax.experimental import pallas as pl
from jax.experimental.pallas import tpu as pltpu
from jax.sharding import PartitionSpec as P

EPSILON = 1e-05
F32 = jnp.float32
BF16 = jnp.bfloat16
NT = (((1,), (1,)), ((), ()))
TN = (((0,), (0,)), ((), ()))
MIB = 1024 * 1024


def iota(shape, dim):
    return lax.broadcasted_iota(jnp.int32, shape, dim)


def dot(a, b):
    return jnp.dot(a, b, preferred_element_type=F32)


def spread(rows, row_key, weight, columns, column_key, keep):
    left = (row_key(iota((rows, weight.shape[0]), 0)) == iota((rows, weight.shape[0]), 1)).astype(BF16)
    right = (column_key(iota((weight.shape[1], columns), 1)) == iota((weight.shape[1], columns), 0)).astype(BF16)
    full = dot(dot(left, weight).astype(BF16), right)
    at = iota((rows, columns), 0), iota((rows, columns), 1)
    return jnp.where(keep(*at), full, 0.0).astype(BF16)


def fetch(sources, targets, sems):
    copies = [pltpu.make_async_copy(s, t, sems.at[n]) for n, (s, t) in enumerate(zip(sources, targets, strict=True))]
    for copy in copies:
        copy.start()
    return copies


def add_embedding(state_ref, index_ref, table, kinds, features, write):
    tokens = index_ref.shape[0]
    group = table.shape[0] // kinds
    spread_tokens = (iota((tokens, tokens * kinds), 1) // kinds == iota((tokens, tokens * kinds), 0)).astype(BF16)
    wide = lax.dot_general(
        index_ref[...].astype(F32).astype(BF16), spread_tokens, TN, preferred_element_type=F32
    )
    onehot = (wide == (iota(wide.shape, 1) % kinds).astype(F32)).astype(BF16)
    width = group * features
    for n in range(tokens // group):
        rows = dot(onehot[:, n * group * kinds : (n + 1) * group * kinds], table)
        write(n * width, (state_ref[:, n * width : (n + 1) * width].astype(F32) + rows).astype(BF16))


def embed_own_kernel(
    state_hbm, index_hbm, table_hbm, out_ref, wide_ref, state_ref, index_ref, table_ref, sems
):
    copies = fetch((index_hbm, table_hbm, state_hbm), (index_ref, table_ref, state_ref), sems)
    kinds, features = table_ref.shape
    copies[1].wait()
    wide_ref[...] = spread(
        wide_ref.shape[0],
        lambda r: r % kinds,
        table_ref[...],
        wide_ref.shape[1],
        lambda c: c % features,
        lambda r, c: r // kinds == c // features,
    )
    copies[0].wait()
    copies[2].wait()

    def write(at, value):
        out_ref[:, at : at + value.shape[1]] = value

    add_embedding(state_ref, index_ref, wide_ref[...], kinds, features, write)


def embed_couple_kernel(kinds, place_ref, own_ref, wide_ref, state_ref, index_ref, out_ref):
    width = own_ref.shape[1]
    place = place_ref[4]
    out_ref[:, pl.ds(pl.multiple_of(place * width, width), width)] = own_ref[...]
    first = pl.multiple_of((1 - place) * width, width)

    def write(at, value):
        out_ref[:, pl.ds(pl.multiple_of(first + at, value.shape[1]), value.shape[1])] = value

    add_embedding(state_ref, index_ref, wide_ref[...], kinds, width // index_ref.shape[0], write)


def weights_kernel(
    place_ref,
    kinds_hbm,
    first_hbm,
    second_hbm,
    outer_hbm,
    bias_hbm,
    mask_hbm,
    pair_hbm,
    gate_up_hbm,
    down_hbm,
    left_hbm,
    right_hbm,
    gain_hbm,
    distance_hbm,
    last_hbm,
    first_out,
    mask_out,
    base_out,
    outer_out,
    pair_out,
    gate_up_out,
    down_out,
    gain_out,
    left_out,
    right_out,
    distance_out,
    last_out,
    kinds_ref,
    first_ref,
    second_ref,
    outer_ref,
    bias_ref,
    mask_ref,
    left_ref,
    right_ref,
    distance_ref,
    last_ref,
    wide,
    rows,
    sems,
):
    copies = fetch(
        (left_hbm, right_hbm, kinds_hbm, first_hbm, second_hbm, bias_hbm, mask_hbm, distance_hbm, last_hbm)
        + (outer_hbm, pair_hbm, gate_up_hbm, down_hbm, gain_hbm),
        (left_ref, right_ref, kinds_ref, first_ref, second_ref, bias_ref, mask_ref, distance_ref, last_ref)
        + (outer_ref, pair_out, gate_up_out, down_out, gain_out),
        sems,
    )
    channels = outer_ref.shape[1]
    length = first_out.shape[0]
    side = left_hbm.shape[1]
    steps = outer_ref.shape[0] // side
    for copy in copies[:9]:
        copy.wait()
    features, c_width = left_ref.shape
    lanes = 4 * c_width
    left_out[...] = spread(
        8 * features,
        lambda r: r % features,
        left_ref[...],
        4 * lanes,
        lambda c: c % c_width,
        lambda r, c: r // features == 2 * (c // lanes) + c % (lanes // 2) // c_width,
    )
    e_width = right_ref.shape[1]
    turned = lax.dot_general(
        (iota((8 * e_width, e_width), 0) // 8 == iota((8 * e_width, e_width), 1)).astype(BF16),
        right_ref[...],
        NT,
        preferred_element_type=F32,
    ).astype(BF16)
    repeat = (iota((features, 8 * features), 1) % features == iota((features, 8 * features), 0)).astype(BF16)
    shape = right_out.shape
    right_out[...] = jnp.where(
        iota(shape, 0) % 8 == iota(shape, 1) // features, dot(turned, repeat), 0.0
    ).astype(BF16)
    weight = distance_ref[...]
    none = jnp.zeros_like(weight)
    distance_out[...] = jnp.concatenate(
        [jnp.concatenate([weight, none], axis=1), jnp.concatenate([none, weight], axis=1)], axis=0
    )
    last_out[...] = jnp.concatenate([last_ref[...], last_ref[...]], axis=1)
    kinds = kinds_ref[...]
    onehot = (iota((first_ref.shape[0], kinds.shape[1]), 0) == kinds).astype(BF16)
    rows[...] = lax.dot_general(onehot, first_ref[...], TN, preferred_element_type=F32)
    first_out[...] = rows[pl.ds(pl.multiple_of(place_ref[3] * length, length), length), :]
    rows[...] = lax.dot_general(onehot, second_ref[...], TN, preferred_element_type=F32)
    second = rows[pl.ds(pl.multiple_of(place_ref[2] * length, length), length), :]
    blocks, columns = mask_ref.shape
    reach = (iota((length, columns), 0) // (length // columns) == iota((length, columns), 1)).astype(BF16)
    mask = lax.dot_general(
        reach, mask_ref[...].astype(F32).astype(BF16), NT, preferred_element_type=F32
    )
    bias = bias_ref[...].astype(F32)
    for b in range(blocks):
        part = jnp.broadcast_to(mask[:, b : b + 1], (length, channels))
        mask_out[b] = part
        base_out[b] = second + part * bias
    copies[9].wait()
    wide[...] = outer_ref[...].astype(F32)
    zero = jnp.zeros((side, channels), BF16)
    for e in range(steps):
        part = wide[pl.ds(e, side, stride=steps), :].astype(BF16)
        outer_out[pl.ds(2 * e * side, side), :] = jnp.concatenate([part, zero], axis=1)
        outer_out[pl.ds((2 * e + 1) * side, side), :] = jnp.concatenate([zero, part], axis=1)
    for copy in copies[10:]:
        copy.wait()


def project_kernel(couples, features, place_ref, *refs):
    parts, weight_ref, right_out, whole = refs[:couples], refs[couples], refs[couples + 1], refs[couples + 2]
    depth, width = parts[0].shape
    for k, part in enumerate(parts):
        couple = lax.rem(place_ref[1] + k, couples)
        whole[:, pl.ds(pl.multiple_of(couple * width, width), width)] = part[...]
    tokens = couples * width // features
    group = weight_ref.shape[1]
    low = iota((8, 2 * depth), 1) < depth
    for t in range(0, tokens // 8, 2):
        sides = []
        for u in (t, t + 1):
            part = whole[:, u * group : (u + 1) * group]
            twice = jnp.concatenate([part, part], axis=0)
            sides.append(lax.dot_general(weight_ref[...], twice, NT, preferred_element_type=F32))
        for g in range(weight_ref.shape[0] // 16):
            rows = [
                jnp.where(low, s[16 * g : 16 * g + 8], s[16 * g + 8 : 16 * g + 16]) for s in sides
            ]
            right_out[pl.ds(g * tokens + t * 8, 16), :] = jnp.concatenate(rows, axis=0).astype(BF16)


def row_of(couple, couples, piece, rows, couple_rows):
    return pl.multiple_of(lax.rem(couple, couples) * couple_rows + piece * rows, rows)


def pair_kernel(
    k,
    piece,
    couples,
    place_ref,
    left_ref,
    left_weight_ref,
    right_ref,
    pair_ref,
    first_ref,
    mask_ref,
    base_ref,
    gain_ref,
    outer_ref,
    gate_up_ref,
    down_ref,
    distance_ref,
    *rest,
):
    pair_out, dist_out, outer, start = rest[-4:]
    rows, length, channels = pair_out.shape
    block_rows = length // mask_ref.shape[0]
    first_row = row_of(place_ref[0] + k, couples, piece, rows, length // couples)
    pairs = rows // 2
    depth, lanes = right_ref.shape[1] // 2, right_ref.shape[1]
    groups = right_ref.shape[0] // length
    hid = down_ref.shape[0]
    bins = distance_ref.shape[0] // 2
    group, columns = left_weight_ref.shape
    half = iota((depth, columns), 1) % lanes < lanes // 2
    weights = []
    for t in range(rows // 8):
        at = (piece * rows // 8 + t) * group
        both = dot(left_ref[:, at : at + group], left_weight_ref[...])
        weights.append(
            jnp.concatenate([jnp.where(half, both, 0.0), jnp.where(half, 0.0, both)], axis=0).astype(BF16)
        )
    for p in range(0, pairs, 2):
        weight = weights[p // 4][:, p % 4 * lanes : (p % 4 + 2) * lanes]
        for g in range(0, groups, 4):
            got = dot(right_ref[g * length : (g + 4) * length, :], weight).astype(BF16)
            for q in range(2):
                for h in range(4):
                    outer[(p + q) * length : (p + q + 1) * length, (g + h) * lanes : (g + h + 1) * lanes] = got[
                        h * length : (h + 1) * length, q * lanes : (q + 1) * lanes
                    ]
    half = outer.shape[0] // 2
    update = [dot(outer[n * half : (n + 1) * half], outer_ref[...]) for n in range(2)]
    first = first_ref[pl.ds(first_row, rows), :]
    for p in range(pairs):
        block = lax.div(first_row + 2 * p, block_rows)
        mask = mask_ref[block] * (1.0 / depth)
        base = base_ref[block]
        at = p * length % half
        part = update[p * length // half][at : at + length]
        for q in range(2):
            i = 2 * p + q
            start[q, p * length : (p + 1) * length, :] = (
                pair_ref[first_row + i].astype(F32)
                + (first[i : i + 1, :] + base)
                + mask * part[:, q * channels : (q + 1) * channels]
            )
    half = min(start.shape[1], 512)
    for q, at in ((q, slice(n, n + half)) for q in range(2) for n in range(0, start.shape[1], half)):
        value = start[q, at]
        mean = jnp.mean(value, axis=-1, keepdims=True)
        centered = value - mean
        variance = jnp.mean(centered * centered, axis=-1, keepdims=True)
        normed = (centered * lax.rsqrt(variance + EPSILON) * gain_ref[...]).astype(BF16)
        gate_up = dot(normed, gate_up_ref[...])
        gate, up = gate_up[:, :hid], gate_up[:, hid:]
        hidden = (0.5 * gate * (1.0 + jnp.tanh(0.5 * gate)) * up).astype(BF16)
        start[q, at] = value + dot(hidden, down_ref[...])
    result = [start[q].astype(BF16) for q in range(2)]
    for p in range(pairs):
        for q in range(2):
            pair_out[2 * p + q] = result[q][p * length : (p + 1) * length]
    dist = lax.dot_general(
        jnp.concatenate(result, axis=1), distance_ref[...], NT, preferred_element_type=F32
    ).astype(BF16)
    for p in range(pairs):
        dist_out[:, 2 * p * bins : 2 * (p + 1) * bins] = dist[p * length : (p + 1) * length]


def own_kernel(couples, pieces, place_ref, *refs):
    count = couples * pieces
    parts, dists = refs[:count], refs[count : 2 * count]
    pair_out, own_ref, sems = refs[2 * count :]
    rows, length, _ = parts[0].shape
    firsts = [
        row_of(place_ref[0] + n // pieces, couples, n % pieces, rows, length // couples)
        for n in range(count)
    ]
    copies = fetch(parts, [pair_out.at[pl.ds(first, rows)] for first in firsts], sems)
    pairs = rows // 2
    lanes = dists[0].shape[1] // pairs
    low = iota((pairs, lanes), 1) < lanes // 2
    for first, dist in zip(firsts, dists, strict=True):
        tiles = jnp.stack([dist[:, p * lanes : (p + 1) * lanes].astype(F32) for p in range(pairs)])
        turned = jnp.swapaxes(tiles, 0, 1)
        for j in range(0, length, 2):
            one, two = turned[j], turned[j + 1]
            own_ref[j // 2, pl.ds(first, pairs, stride=2), :] = jnp.where(
                low, one, pltpu.roll(two, lanes // 2, 1)
            )
            own_ref[j // 2, pl.ds(first + 1, pairs, stride=2), :] = jnp.where(
                low, pltpu.roll(one, lanes // 2, 1), two
            )
    for copy in copies:
        copy.wait()


def final_kernel(couples, pieces, place_ref, own_ref, bias_ref, *refs):
    count = couples * pieces
    out_ref = refs[count]
    lanes = bias_ref.shape[1]
    length = out_ref.shape[0]
    tiles = refs[0].shape[1] // lanes
    for n in range(count):
        first = lax.rem(place_ref[1] + n // pieces, couples) * (pieces * tiles) + n % pieces * tiles
        for t in range(tiles):
            value = own_ref[first + t] + refs[n][:, t * lanes : (t + 1) * lanes].astype(F32) + bias_ref[...]
            out_ref[:, pl.ds(pl.multiple_of((first + t) * lanes, lanes), lanes)] = value.astype(BF16)


COST = pl.CostEstimate(flops=0, bytes_accessed=0, transcendentals=0)


def params(mib):
    return pltpu.CompilerParams(vmem_limit_bytes=mib * MIB)


def in_hbm(*arrays):
    return [pltpu.with_memory_space_constraint(a, pltpu.HBM) for a in arrays]


VMEM = pl.BlockSpec(memory_space=pltpu.VMEM)
SMEM = pl.BlockSpec(memory_space=pltpu.SMEM)
HBM = pl.BlockSpec(memory_space=pltpu.HBM)


def local(
    row_count,
    col_count,
    pair_state,
    token_kinds,
    first_type_table,
    second_type_table,
    alignment_state,
    alignment_index,
    alignment_table,
    first_weight,
    second_weight,
    outer_product_weight,
    outer_product_bias,
    pair_block_mask,
    transition_gain,
    transition_gate_up,
    transition_down,
    distance_weight,
    distance_bias,
):
    length = pair_state.shape[0]
    channels = pair_state.shape[2]
    depth = alignment_index.shape[0]
    features, c_width = first_weight.shape
    e_width = second_weight.shape[1]
    bins = distance_weight.shape[1]
    axes = ("row", "col")
    row, col = lax.axis_index("row"), lax.axis_index("col")
    place = jnp.stack([col // 2, row // 2, col, row, col % 2]).astype(jnp.int32)
    couples = col_count // 2

    def moved(value, target):
        pairs = [
            (r * col_count + c, target(r, c)[0] * col_count + target(r, c)[1])
            for r in range(row_count)
            for c in range(col_count)
        ]
        return lax.ppermute(value, axes, pairs)

    turned_index = alignment_index.T
    other_index = moved(turned_index, lambda r, c: (r, c ^ 1))
    other_state = moved(alignment_state, lambda r, c: (r, c ^ 1))
    couple = (alignment_state.shape[0], 2 * alignment_state.shape[1])
    kinds = alignment_table.shape[0]
    group = min(alignment_index.shape[1], 256 // features)
    own_embedded, wide_table = pl.pallas_call(
        embed_own_kernel,
        out_shape=(
            jax.ShapeDtypeStruct(alignment_state.shape, BF16),
            jax.ShapeDtypeStruct((group * kinds, group * features), BF16),
        ),
        in_specs=[HBM] * 3,
        out_specs=(VMEM,) * 2,
        scratch_shapes=[
            pltpu.VMEM(alignment_state.shape, BF16),
            pltpu.VMEM(turned_index.shape, jnp.int32),
            pltpu.VMEM(alignment_table.shape, BF16),
            pltpu.SemaphoreType.DMA((3,)),
        ],
        compiler_params=params(4),
        cost_estimate=COST,
        name="embed_own",
    )(*in_hbm(alignment_state, turned_index, alignment_table))
    embedded = pl.pallas_call(
        functools.partial(embed_couple_kernel, kinds),
        out_shape=jax.ShapeDtypeStruct(couple, BF16),
        in_specs=[SMEM] + [VMEM] * 4,
        out_specs=VMEM,
        compiler_params=params(4),
        cost_estimate=COST,
        name="embed_couple",
    )(place, own_embedded, wide_table, other_state, other_index)

    rights = [
        moved(embedded, lambda r, c, k=k: ((c - 2 * k) % row_count, r)) for k in range(couples)
    ]
    lefts = [embedded] + [
        moved(embedded, lambda r, c, k=k: (r, (c - 2 * k) % col_count)) for k in range(1, couples)
    ]

    blocks = pair_block_mask.shape[0]
    maps = jax.ShapeDtypeStruct((blocks, length, channels), F32)
    first_rows, masks, bases, outer_weight, pair_in, gate_up, down, gain, left_weight, right_weight, turned_distance, last = pl.pallas_call(
        weights_kernel,
        out_shape=(
            jax.ShapeDtypeStruct((length, channels), F32),
            maps,
            maps,
            jax.ShapeDtypeStruct((2 * c_width * e_width, 2 * channels), BF16),
            jax.ShapeDtypeStruct(pair_state.shape, BF16),
            jax.ShapeDtypeStruct(transition_gate_up.shape, BF16),
            jax.ShapeDtypeStruct(transition_down.shape, BF16),
            jax.ShapeDtypeStruct((1, channels), F32),
            jax.ShapeDtypeStruct((8 * features, 16 * c_width), BF16),
            jax.ShapeDtypeStruct((8 * e_width, 8 * features), BF16),
            jax.ShapeDtypeStruct((2 * bins, 2 * channels), BF16),
            jax.ShapeDtypeStruct((1, 2 * bins), F32),
        ),
        in_specs=[SMEM] + [HBM] * 14,
        out_specs=(VMEM,) * 12,
        scratch_shapes=[
            pltpu.VMEM((1, token_kinds.shape[0]), jnp.int32),
            pltpu.VMEM(first_type_table.shape, BF16),
            pltpu.VMEM(second_type_table.shape, BF16),
            pltpu.VMEM(outer_product_weight.shape, BF16),
            pltpu.VMEM((1, channels), BF16),
            pltpu.VMEM(pair_block_mask.shape, jnp.int32),
            pltpu.VMEM(first_weight.shape, BF16),
            pltpu.VMEM(second_weight.shape, BF16),
            pltpu.VMEM((bins, channels), BF16),
            pltpu.VMEM((1, bins), F32),
            pltpu.VMEM(outer_product_weight.shape, F32),
            pltpu.VMEM((token_kinds.shape[0], channels), F32),
            pltpu.SemaphoreType.DMA((14,)),
        ],
        compiler_params=params(8),
        cost_estimate=COST,
        name="weights",
    )(
        place,
        *in_hbm(
            token_kinds.reshape(1, -1),
            first_type_table,
            second_type_table,
            outer_product_weight,
            outer_product_bias.reshape(1, -1),
            pair_block_mask,
            pair_state,
            transition_gate_up,
            transition_down,
            first_weight,
            second_weight,
            transition_gain.reshape(1, -1),
            distance_weight.T,
            distance_bias.reshape(1, -1),
        ),
    )

    right_tiles = pl.pallas_call(
        functools.partial(project_kernel, couples, features),
        out_shape=jax.ShapeDtypeStruct((e_width // 2 * length, 2 * depth), BF16),
        in_specs=[SMEM] + [VMEM] * (couples + 1),
        out_specs=VMEM,
        scratch_shapes=[pltpu.VMEM((depth, couples * couple[1]), BF16)],
        compiler_params=params(8),
        cost_estimate=COST,
        name="project",
    )(place, *rights, right_weight)

    couple_rows = length // couples
    pieces = 1
    rows = couple_rows // pieces
    pair_parts, dist_parts, crossed, mirror_parts = [], [], [], []
    for n in range(couples * pieces):
        before = dist_parts[-1:] if n else lefts[1:]
        if n >= 2:
            before = before + (crossed[-1:] if n % 2 == 0 else mirror_parts[n - 3 : n - 1])
        pair_part, dist_part = pl.pallas_call(
            functools.partial(pair_kernel, n // pieces, n % pieces, couples),
            out_shape=(
                jax.ShapeDtypeStruct((rows, length, channels), BF16),
                jax.ShapeDtypeStruct((length, rows * bins), BF16),
            ),
            in_specs=[SMEM] + [VMEM] * (12 + len(before)),
            out_specs=(VMEM,) * 2,
            scratch_shapes=[
                pltpu.VMEM((rows // 2 * length, 2 * c_width * e_width), BF16),
                pltpu.VMEM((2, rows // 2 * length, channels), F32),
            ],
            compiler_params=params(16),
            cost_estimate=COST,
            name="pairs",
        )(
            place,
            lefts[n // pieces],
            left_weight,
            right_tiles,
            pair_in,
            first_rows,
            masks,
            bases,
            gain,
            outer_weight,
            gate_up,
            down,
            turned_distance,
            *before,
        )
        pair_parts.append(pair_part)
        dist_parts.append(dist_part)
        if n % 2 == 0:
            crossed.append(moved(dist_part, lambda r, c: (r, (c + col_count // 2) % col_count)))
            mirror_parts.append(moved(crossed[-1], lambda r, c: ((c + col_count // 2) % col_count, r)))
        else:
            mirror_parts.append(moved(dist_part, lambda r, c: (c, r)))
    pair_out, own = pl.pallas_call(
        functools.partial(own_kernel, couples, pieces),
        out_shape=(
            jax.ShapeDtypeStruct(pair_state.shape, BF16),
            jax.ShapeDtypeStruct((length // 2, length, 2 * bins), F32),
        ),
        in_specs=[SMEM] + [VMEM] * (2 * len(pair_parts)),
        out_specs=(HBM, VMEM),
        scratch_shapes=[pltpu.SemaphoreType.DMA((len(pair_parts),))],
        compiler_params=params(8),
        cost_estimate=COST,
        name="own",
    )(place, *pair_parts, *dist_parts)
    distogram = pl.pallas_call(
        functools.partial(final_kernel, couples, pieces),
        out_shape=jax.ShapeDtypeStruct((length, length * bins), BF16),
        in_specs=[SMEM] + [VMEM] * (len(mirror_parts) + 2),
        out_specs=VMEM,
        compiler_params=params(8),
        cost_estimate=COST,
        name="final",
    )(place, own, last, *mirror_parts)
    return pair_out, distogram


def solution(mesh):
    split = P(("conf", "row"), "col")
    tokens = P(None, ("conf", "row", "col"))
    in_specs = (
        P(("conf", "row"), "col", None),
        P("conf"),
        P(),
        P(),
        tokens,
        tokens,
        P(),
        P(),
        P(),
        P(),
        P(),
        split,
        P(),
        P(),
        P(),
        P(),
        P(),
    )
    return jax.shard_map(
        functools.partial(local, mesh.shape["row"], mesh.shape["col"]),
        mesh=mesh,
        in_specs=in_specs,
        out_specs=(P(("conf", "row"), "col", None), split),
        check_vma=False,
    )
```

```python
import functools

import jax
import jax.numpy as jnp
from jax import lax
from jax.experimental import pallas as pl
from jax.experimental.pallas import tpu as pltpu
from jax.sharding import PartitionSpec as P

EPSILON = 1e-05
F32 = jnp.float32
BF16 = jnp.bfloat16
NT = (((1,), (1,)), ((), ()))
TN = (((0,), (0,)), ((), ()))
MIB = 1024 * 1024
ORDER = (1, 0)


def iota(shape, dim):
    return lax.broadcasted_iota(jnp.int32, shape, dim)


def dot(a, b):
    return jnp.dot(a, b, preferred_element_type=F32)


def spread(rows, row_key, weight, columns, column_key, keep):
    left = (row_key(iota((rows, weight.shape[0]), 0)) == iota((rows, weight.shape[0]), 1)).astype(BF16)
    right = (column_key(iota((weight.shape[1], columns), 1)) == iota((weight.shape[1], columns), 0)).astype(BF16)
    full = dot(dot(left, weight).astype(BF16), right)
    at = iota((rows, columns), 0), iota((rows, columns), 1)
    return jnp.where(keep(*at), full, 0.0).astype(BF16)


def fetch(sources, targets, sems):
    copies = [pltpu.make_async_copy(s, t, sems.at[n]) for n, (s, t) in enumerate(zip(sources, targets, strict=True))]
    for copy in copies:
        copy.start()
    return copies


def add_embedding(state_ref, index_ref, table, kinds, features, write):
    tokens = index_ref.shape[0]
    group = table.shape[0] // kinds
    spread_tokens = (iota((tokens, tokens * kinds), 1) // kinds == iota((tokens, tokens * kinds), 0)).astype(BF16)
    wide = lax.dot_general(
        index_ref[...].astype(F32).astype(BF16), spread_tokens, TN, preferred_element_type=F32
    )
    onehot = (wide == (iota(wide.shape, 1) % kinds).astype(F32)).astype(BF16)
    width = group * features
    for n in range(tokens // group):
        rows = dot(onehot[:, n * group * kinds : (n + 1) * group * kinds], table)
        write(n * width, (state_ref[:, n * width : (n + 1) * width].astype(F32) + rows).astype(BF16))


def embed_own_kernel(
    state_hbm, index_hbm, table_hbm, out_ref, wide_ref, state_ref, index_ref, table_ref, sems
):
    copies = fetch((index_hbm, table_hbm, state_hbm), (index_ref, table_ref, state_ref), sems)
    kinds, features = table_ref.shape
    copies[1].wait()
    wide_ref[...] = spread(
        wide_ref.shape[0],
        lambda r: r % kinds,
        table_ref[...],
        wide_ref.shape[1],
        lambda c: c % features,
        lambda r, c: r // kinds == c // features,
    )
    copies[0].wait()
    copies[2].wait()

    def write(at, value):
        out_ref[:, at : at + value.shape[1]] = value

    add_embedding(state_ref, index_ref, wide_ref[...], kinds, features, write)


def embed_group_kernel(kinds, size, place_ref, own_ref, wide_ref, *refs):
    states, indices, out_ref = refs[: size - 1], refs[size - 1 : 2 * size - 2], refs[2 * size - 2]
    width = own_ref.shape[1]
    position = place_ref[4]
    out_ref[:, pl.ds(pl.multiple_of(position * width, width), width)] = own_ref[...]
    for n, (state, index) in enumerate(zip(states, indices, strict=True)):
        first = lax.rem(position + n + 1, size) * width

        def write(at, value, first=first):
            out_ref[:, pl.ds(pl.multiple_of(first + at, value.shape[1]), value.shape[1])] = value

        add_embedding(state, index, wide_ref[...], kinds, width // index.shape[0], write)


def weights_kernel(
    place_ref,
    kinds_hbm,
    first_hbm,
    second_hbm,
    outer_hbm,
    bias_hbm,
    mask_hbm,
    pair_hbm,
    gate_up_hbm,
    down_hbm,
    left_hbm,
    right_hbm,
    gain_hbm,
    distance_hbm,
    last_hbm,
    embedded_ref,
    first_out,
    mask_out,
    base_out,
    outer_out,
    pair_out,
    gate_up_out,
    down_out,
    gain_out,
    left_out,
    right_out,
    distance_out,
    last_out,
    tiles_out,
    kinds_ref,
    first_ref,
    second_ref,
    outer_ref,
    bias_ref,
    mask_ref,
    left_ref,
    right_ref,
    distance_ref,
    last_ref,
    wide,
    rows,
    sems,
):
    copies = fetch(
        (left_hbm, right_hbm, kinds_hbm, first_hbm, second_hbm, bias_hbm, mask_hbm, distance_hbm, last_hbm)
        + (outer_hbm, pair_hbm, gate_up_hbm, down_hbm, gain_hbm),
        (left_ref, right_ref, kinds_ref, first_ref, second_ref, bias_ref, mask_ref, distance_ref, last_ref)
        + (outer_ref, pair_out, gate_up_out, down_out, gain_out),
        sems,
    )
    channels = outer_ref.shape[1]
    length = first_out.shape[0]
    side = left_hbm.shape[1]
    steps = outer_ref.shape[0] // side
    for copy in copies[:9]:
        copy.wait()
    features, c_width = left_ref.shape
    lanes = 4 * c_width
    left_out[...] = spread(
        8 * features,
        lambda r: r % features,
        left_ref[...],
        4 * lanes,
        lambda c: c % c_width,
        lambda r, c: r // features == 2 * (c // lanes) + c % (lanes // 2) // c_width,
    )
    project_left(place_ref, [(0, embedded_ref)], left_out, tiles_out)
    e_width = right_ref.shape[1]
    turned = lax.dot_general(
        (iota((8 * e_width, e_width), 0) // 8 == iota((8 * e_width, e_width), 1)).astype(BF16),
        right_ref[...],
        NT,
        preferred_element_type=F32,
    ).astype(BF16)
    repeat = (iota((features, 8 * features), 1) % features == iota((features, 8 * features), 0)).astype(BF16)
    shape = right_out.shape
    right_out[...] = jnp.where(
        iota(shape, 0) % 8 == iota(shape, 1) // features, dot(turned, repeat), 0.0
    ).astype(BF16)
    weight = distance_ref[...]
    none = jnp.zeros_like(weight)
    distance_out[...] = jnp.concatenate(
        [jnp.concatenate([weight, none], axis=1), jnp.concatenate([none, weight], axis=1)], axis=0
    )
    last_out[...] = jnp.concatenate([last_ref[...], last_ref[...]], axis=1)
    kinds = kinds_ref[...]
    onehot = (iota((first_ref.shape[0], kinds.shape[1]), 0) == kinds).astype(BF16)
    rows[...] = lax.dot_general(onehot, first_ref[...], TN, preferred_element_type=F32)
    first_out[...] = rows[pl.ds(pl.multiple_of(place_ref[3] * length, length), length), :]
    rows[...] = lax.dot_general(onehot, second_ref[...], TN, preferred_element_type=F32)
    second = rows[pl.ds(pl.multiple_of(place_ref[2] * length, length), length), :]
    blocks, columns = mask_ref.shape
    reach = (iota((length, columns), 0) // (length // columns) == iota((length, columns), 1)).astype(BF16)
    mask = lax.dot_general(
        reach, mask_ref[...].astype(F32).astype(BF16), NT, preferred_element_type=F32
    )
    bias = bias_ref[...].astype(F32)
    for b in range(blocks):
        part = jnp.broadcast_to(mask[:, b : b + 1], (length, channels))
        mask_out[b] = part
        base_out[b] = second + part * bias
    copies[9].wait()
    wide[...] = outer_ref[...].astype(F32)
    zero = jnp.zeros((side, channels), BF16)
    for e in range(steps):
        part = wide[pl.ds(e, side, stride=steps), :].astype(BF16)
        outer_out[pl.ds(2 * e * side, side), :] = jnp.concatenate([part, zero], axis=1)
        outer_out[pl.ds((2 * e + 1) * side, side), :] = jnp.concatenate([zero, part], axis=1)
    for copy in copies[10:]:
        copy.wait()


def project_left(place_ref, parts, weight_ref, out_ref):
    group, columns = weight_ref.shape
    depth, width = parts[0][1].shape
    lanes = columns // 4
    half = iota((depth, columns), 1) % lanes < lanes // 2
    for k, part in parts:
        first = lax.rem(place_ref[0] + k, 2) * (width // group * columns)
        for t in range(width // group):
            both = dot(part[:, t * group : (t + 1) * group], weight_ref[...])
            at = pl.ds(pl.multiple_of(first + t * columns, columns), columns)
            out_ref[0:depth, at] = jnp.where(half, both, 0.0).astype(BF16)
            out_ref[depth : 2 * depth, at] = jnp.where(half, 0.0, both).astype(BF16)


def project_right(part_ref, weight_ref, out_ref):
    depth, width = part_ref.shape
    group = weight_ref.shape[1]
    tokens = width // group * 8
    low = iota((8, 2 * depth), 1) < depth
    for t in range(0, tokens // 8, 2):
        sides = []
        for u in (t, t + 1):
            part = part_ref[:, u * group : (u + 1) * group]
            twice = jnp.concatenate([part, part], axis=0)
            sides.append(lax.dot_general(weight_ref[...], twice, NT, preferred_element_type=F32))
        for g in range(weight_ref.shape[0] // 16):
            rows = [
                jnp.where(low, s[16 * g : 16 * g + 8], s[16 * g + 8 : 16 * g + 16]) for s in sides
            ]
            out_ref[pl.ds(g * tokens + t * 8, 16), :] = jnp.concatenate(rows, axis=0).astype(BF16)


def project_both_kernel(
    place_ref, other_ref, right_ref, left_weight_ref, right_weight_ref, left_in, left_out, right_out
):
    del left_in
    project_right(right_ref, right_weight_ref, right_out)
    project_left(place_ref, [(1, other_ref)], left_weight_ref, left_out)


def project_right_kernel(right_ref, right_weight_ref, right_out):
    project_right(right_ref, right_weight_ref, right_out)


def half_of(place, k, size):
    return pl.multiple_of(lax.rem(place + k, 2) * size, size)


def pair_kernel(
    k,
    place_ref,
    left_ref,
    right_ref,
    pair_ref,
    first_ref,
    mask_ref,
    base_ref,
    gain_ref,
    outer_ref,
    gate_up_ref,
    down_ref,
    distance_ref,
    *rest,
):
    pair_out, dist_out, outer, start = rest[-4:]
    length, size, channels = pair_out.shape
    block_rows = length // mask_ref.shape[0]
    second = pl.ds(half_of(place_ref[1], k, size), size)
    pairs = length // 2
    depth, lanes = right_ref.shape[1] // 2, right_ref.shape[1]
    groups = right_ref.shape[0] // size
    step = min(groups, 256 // size)
    hid = down_ref.shape[0]
    bins = distance_ref.shape[0] // 2
    for p in range(0, pairs, 2):
        weight = left_ref[:, p * lanes : (p + 2) * lanes]
        for g in range(0, groups, step):
            got = dot(right_ref[g * size : (g + step) * size, :], weight).astype(BF16)
            for q in range(2):
                for h in range(step):
                    outer[(p + q) * size : (p + q + 1) * size, (g + h) * lanes : (g + h + 1) * lanes] = got[
                        h * size : (h + 1) * size, q * lanes : (q + 1) * lanes
                    ]
    part_rows = max(size, outer.shape[0] // 8)
    update = [
        dot(outer[n : n + part_rows], outer_ref[...]) for n in range(0, outer.shape[0], part_rows)
    ]
    for p in range(pairs):
        block = 2 * p // block_rows
        mask = mask_ref[block, second, :] * (1.0 / depth)
        base = base_ref[block, second, :]
        at = p * size % part_rows
        part = update[p * size // part_rows][at : at + size]
        for q in range(2):
            i = 2 * p + q
            start[q, p * size : (p + 1) * size, :] = (
                pair_ref[i, second, :].astype(F32)
                + (first_ref[i : i + 1, :] + base)
                + mask * part[:, q * channels : (q + 1) * channels]
            )
    half = min(start.shape[1], 512)
    for q, at in ((q, slice(n, n + half)) for q in range(2) for n in range(0, start.shape[1], half)):
        value = start[q, at]
        mean = jnp.mean(value, axis=-1, keepdims=True)
        centered = value - mean
        variance = jnp.mean(centered * centered, axis=-1, keepdims=True)
        normed = (centered * lax.rsqrt(variance + EPSILON) * gain_ref[...]).astype(BF16)
        gate_up = dot(normed, gate_up_ref[...])
        gate, up = gate_up[:, :hid], gate_up[:, hid:]
        hidden = (0.5 * gate * (1.0 + jnp.tanh(0.5 * gate)) * up).astype(BF16)
        start[q, at] = value + dot(hidden, down_ref[...])
    result = [start[q].astype(BF16) for q in range(2)]
    for p in range(pairs):
        for q in range(2):
            pair_out[2 * p + q] = result[q][p * size : (p + 1) * size]
    dist = lax.dot_general(
        jnp.concatenate(result, axis=1), distance_ref[...], NT, preferred_element_type=F32
    ).astype(BF16)
    for p in range(pairs):
        dist_out[:, 2 * p * bins : 2 * (p + 1) * bins] = dist[p * size : (p + 1) * size]


def own_kernel(order, place_ref, *refs):
    count = len(order)
    parts, dists = refs[:count], refs[count : 2 * count]
    pair_out, own_ref, sems = refs[2 * count :]
    length, size, _ = parts[0].shape
    firsts = [half_of(place_ref[1], k, size) for k in order]
    copies = fetch(parts, [pair_out.at[:, pl.ds(first, size)] for first in firsts], sems)
    pairs = length // 2
    lanes = dists[0].shape[1] // pairs
    low = iota((pairs, lanes), 1) < lanes // 2
    for k, dist in zip(order, dists, strict=True):
        first = half_of(place_ref[1], k, size // 2)
        tiles = jnp.stack([dist[:, p * lanes : (p + 1) * lanes].astype(F32) for p in range(pairs)])
        turned = jnp.swapaxes(tiles, 0, 1)
        for j in range(0, size, 2):
            one, two = turned[j], turned[j + 1]
            own_ref[first + j // 2, pl.ds(0, pairs, stride=2), :] = jnp.where(
                low, one, pltpu.roll(two, lanes // 2, 1)
            )
            own_ref[first + j // 2, pl.ds(1, pairs, stride=2), :] = jnp.where(
                low, pltpu.roll(one, lanes // 2, 1), two
            )
    for copy in copies:
        copy.wait()


def final_kernel(order, place_ref, own_ref, bias_ref, *refs):
    out_ref = refs[len(order)]
    lanes = bias_ref.shape[1]

    def write(swapped):
        for k, part in zip(order, refs, strict=False):
            size, width = part.shape
            first = (k + swapped) % 2 * size
            rows = slice(first, first + size)
            for t in range(width // lanes):
                at = slice(t * lanes, (t + 1) * lanes)
                value = own_ref[t, rows, :] + part[:, at].astype(F32) + bias_ref[...]
                out_ref[rows, at] = value.astype(BF16)

    pl.when(place_ref[0] == 0)(functools.partial(write, 0))
    pl.when(place_ref[0] == 1)(functools.partial(write, 1))


PAIR_COST = pl.CostEstimate(flops=5_000_000_000, bytes_accessed=16_000_000, transcendentals=0)
COST = pl.CostEstimate(flops=0, bytes_accessed=0, transcendentals=0)


def params(mib):
    return pltpu.CompilerParams(vmem_limit_bytes=mib * MIB)


def in_hbm(*arrays):
    return [pltpu.with_memory_space_constraint(a, pltpu.HBM) for a in arrays]


VMEM = pl.BlockSpec(memory_space=pltpu.VMEM)
SMEM = pl.BlockSpec(memory_space=pltpu.SMEM)
HBM = pl.BlockSpec(memory_space=pltpu.HBM)


def local(
    row_count,
    col_count,
    pair_state,
    token_kinds,
    first_type_table,
    second_type_table,
    alignment_state,
    alignment_index,
    alignment_table,
    first_weight,
    second_weight,
    outer_product_weight,
    outer_product_bias,
    pair_block_mask,
    transition_gain,
    transition_gate_up,
    transition_down,
    distance_weight,
    distance_bias,
):
    length = pair_state.shape[0]
    channels = pair_state.shape[2]
    depth = alignment_index.shape[0]
    features, c_width = first_weight.shape
    e_width = second_weight.shape[1]
    bins = distance_weight.shape[1]
    axes = ("row", "col")
    row, col = lax.axis_index("row"), lax.axis_index("col")
    size = col_count // 2
    place = jnp.stack([col // size, row // size, col, row, col % size]).astype(jnp.int32)

    def moved(value, target):
        pairs = [
            (r * col_count + c, target(r, c)[0] * col_count + target(r, c)[1])
            for r in range(row_count)
            for c in range(col_count)
        ]
        return lax.ppermute(value, axes, pairs)

    def neighbour(value, k):
        return moved(value, lambda r, c: (r, c - c % size + (c - k) % size))

    turned_index = alignment_index.T
    other_indices = [neighbour(turned_index, k) for k in range(1, size)]
    other_states = [neighbour(alignment_state, k) for k in range(1, size)]
    kinds = alignment_table.shape[0]
    group = min(alignment_index.shape[1], 256 // features)
    own_embedded, wide_table = pl.pallas_call(
        embed_own_kernel,
        out_shape=(
            jax.ShapeDtypeStruct(alignment_state.shape, BF16),
            jax.ShapeDtypeStruct((group * kinds, group * features), BF16),
        ),
        in_specs=[HBM] * 3,
        out_specs=(VMEM,) * 2,
        scratch_shapes=[
            pltpu.VMEM(alignment_state.shape, BF16),
            pltpu.VMEM(turned_index.shape, jnp.int32),
            pltpu.VMEM(alignment_table.shape, BF16),
            pltpu.SemaphoreType.DMA((3,)),
        ],
        compiler_params=params(4),
        cost_estimate=COST,
        name="embed_own",
    )(*in_hbm(alignment_state, turned_index, alignment_table))
    embedded = pl.pallas_call(
        functools.partial(embed_group_kernel, kinds, size),
        out_shape=jax.ShapeDtypeStruct((depth, size * alignment_state.shape[1]), BF16),
        in_specs=[SMEM] + [VMEM] * (2 * size),
        out_specs=VMEM,
        compiler_params=params(4),
        cost_estimate=COST,
        name="embed_group",
    )(place, own_embedded, wide_table, *other_states, *other_indices)

    rights = {
        k: moved(embedded, lambda r, c, k=k: ((c - size * k) % row_count, r)) for k in ORDER
    }
    other = moved(embedded, lambda r, c: (r, (c + size) % col_count))

    blocks = pair_block_mask.shape[0]
    maps = jax.ShapeDtypeStruct((blocks, length, channels), F32)
    left_shape = jax.ShapeDtypeStruct((2 * depth, 2 * length * c_width), BF16)
    (
        first_rows,
        masks,
        bases,
        outer_weight,
        pair_in,
        gate_up,
        down,
        gain,
        left_weight,
        right_weight,
        turned_distance,
        last,
        left_tiles,
    ) = pl.pallas_call(
        weights_kernel,
        out_shape=(
            jax.ShapeDtypeStruct((length, channels), F32),
            maps,
            maps,
            jax.ShapeDtypeStruct((2 * c_width * e_width, 2 * channels), BF16),
            jax.ShapeDtypeStruct(pair_state.shape, BF16),
            jax.ShapeDtypeStruct(transition_gate_up.shape, BF16),
            jax.ShapeDtypeStruct(transition_down.shape, BF16),
            jax.ShapeDtypeStruct((1, channels), F32),
            jax.ShapeDtypeStruct((8 * features, 16 * c_width), BF16),
            jax.ShapeDtypeStruct((8 * e_width, 8 * features), BF16),
            jax.ShapeDtypeStruct((2 * bins, 2 * channels), BF16),
            jax.ShapeDtypeStruct((1, 2 * bins), F32),
            left_shape,
        ),
        in_specs=[SMEM] + [HBM] * 14 + [VMEM],
        out_specs=(VMEM,) * 13,
        scratch_shapes=[
            pltpu.VMEM((1, token_kinds.shape[0]), jnp.int32),
            pltpu.VMEM(first_type_table.shape, BF16),
            pltpu.VMEM(second_type_table.shape, BF16),
            pltpu.VMEM(outer_product_weight.shape, BF16),
            pltpu.VMEM((1, channels), BF16),
            pltpu.VMEM(pair_block_mask.shape, jnp.int32),
            pltpu.VMEM(first_weight.shape, BF16),
            pltpu.VMEM(second_weight.shape, BF16),
            pltpu.VMEM((bins, channels), BF16),
            pltpu.VMEM((1, bins), F32),
            pltpu.VMEM(outer_product_weight.shape, F32),
            pltpu.VMEM((token_kinds.shape[0], channels), F32),
            pltpu.SemaphoreType.DMA((14,)),
        ],
        compiler_params=params(8),
        cost_estimate=COST,
        name="weights",
    )(
        place,
        *in_hbm(
            token_kinds.reshape(1, -1),
            first_type_table,
            second_type_table,
            outer_product_weight,
            outer_product_bias.reshape(1, -1),
            pair_block_mask,
            pair_state,
            transition_gate_up,
            transition_down,
            first_weight,
            second_weight,
            transition_gain.reshape(1, -1),
            distance_weight.T,
            distance_bias.reshape(1, -1),
        ),
        embedded,
    )

    half = length // 2
    right_shape = jax.ShapeDtypeStruct((e_width // 2 * half, 2 * depth), BF16)
    pair_parts, dist_parts, mirror_parts = [], [], []
    for n, k in enumerate(ORDER):
        if n == 0:
            left_tiles, right_tiles = pl.pallas_call(
                project_both_kernel,
                out_shape=(left_shape, right_shape),
                in_specs=[SMEM] + [VMEM] * 5,
                out_specs=(VMEM,) * 2,
                input_output_aliases={5: 0},
                compiler_params=params(4),
                cost_estimate=COST,
                name="project_both",
            )(place, other, rights[k], left_weight, right_weight, left_tiles)
        else:
            right_tiles = pl.pallas_call(
                project_right_kernel,
                out_shape=right_shape,
                in_specs=[VMEM] * 2,
                out_specs=VMEM,
                compiler_params=params(4),
                cost_estimate=COST,
                name="project_right",
            )(rights[k], right_weight)
        before = dist_parts[-1:]
        pair_part, dist_part = pl.pallas_call(
            functools.partial(pair_kernel, k),
            out_shape=(
                jax.ShapeDtypeStruct((length, half, channels), BF16),
                jax.ShapeDtypeStruct((half, length * bins), BF16),
            ),
            in_specs=[SMEM] + [VMEM] * (11 + len(before)),
            out_specs=(VMEM,) * 2,
            scratch_shapes=[
                pltpu.VMEM((length // 2 * half, 2 * c_width * e_width), BF16),
                pltpu.VMEM((2, length // 2 * half, channels), F32),
            ],
            compiler_params=params(24),
            cost_estimate=PAIR_COST,
            name="pairs",
        )(
            place,
            left_tiles,
            right_tiles,
            pair_in,
            first_rows,
            masks,
            bases,
            gain,
            outer_weight,
            gate_up,
            down,
            turned_distance,
            *before,
        )
        pair_parts.append(pair_part)
        dist_parts.append(dist_part)
        if n == 0:
            crossed = moved(dist_part, lambda r, c: (r, (c + size) % col_count))
            mirror_parts.append(moved(crossed, lambda r, c: ((c + size) % col_count, r)))
        else:
            mirror_parts.append(moved(dist_part, lambda r, c: (c, r)))
    pair_out, own = pl.pallas_call(
        functools.partial(own_kernel, ORDER),
        out_shape=(
            jax.ShapeDtypeStruct(pair_state.shape, BF16),
            jax.ShapeDtypeStruct((length // 2, length, 2 * bins), F32),
        ),
        in_specs=[SMEM] + [VMEM] * (2 * len(pair_parts)),
        out_specs=(HBM, VMEM),
        scratch_shapes=[pltpu.SemaphoreType.DMA((len(pair_parts),))],
        compiler_params=params(8),
        cost_estimate=COST,
        name="own",
    )(place, *pair_parts, *dist_parts)
    distogram = pl.pallas_call(
        functools.partial(final_kernel, ORDER),
        out_shape=jax.ShapeDtypeStruct((length, length * bins), BF16),
        in_specs=[SMEM] + [VMEM] * 4,
        out_specs=VMEM,
        compiler_params=params(4),
        cost_estimate=COST,
        name="final",
    )(place, own, last, *mirror_parts)
    return pair_out, distogram


def solution(mesh):
    split = P(("conf", "row"), "col")
    tokens = P(None, ("conf", "row", "col"))
    in_specs = (
        P(("conf", "row"), "col", None),
        P("conf"),
        P(),
        P(),
        tokens,
        tokens,
        P(),
        P(),
        P(),
        P(),
        P(),
        split,
        P(),
        P(),
        P(),
        P(),
        P(),
    )
    return jax.shard_map(
        functools.partial(local, mesh.shape["row"], mesh.shape["col"]),
        mesh=mesh,
        in_specs=in_specs,
        out_specs=(P(("conf", "row"), "col", None), split),
        check_vma=False,
    )
```

```python
import functools

import jax
import jax.numpy as jnp
from jax import lax
from jax.experimental import pallas as pl
from jax.experimental.pallas import tpu as pltpu
from jax.sharding import PartitionSpec as P

EPSILON = 1e-05
F32 = jnp.float32
BF16 = jnp.bfloat16
NT = (((1,), (1,)), ((), ()))
TN = (((0,), (0,)), ((), ()))
MIB = 1024 * 1024
ORDER = (1, 0)


def iota(shape, dim):
    return lax.broadcasted_iota(jnp.int32, shape, dim)


def dot(a, b):
    return jnp.dot(a, b, preferred_element_type=F32)


def spread(rows, row_key, weight, columns, column_key, keep):
    left = (row_key(iota((rows, weight.shape[0]), 0)) == iota((rows, weight.shape[0]), 1)).astype(BF16)
    right = (column_key(iota((weight.shape[1], columns), 1)) == iota((weight.shape[1], columns), 0)).astype(BF16)
    full = dot(dot(left, weight).astype(BF16), right)
    at = iota((rows, columns), 0), iota((rows, columns), 1)
    return jnp.where(keep(*at), full, 0.0).astype(BF16)


def fetch(sources, targets, sems):
    copies = [pltpu.make_async_copy(s, t, sems.at[n]) for n, (s, t) in enumerate(zip(sources, targets, strict=True))]
    for copy in copies:
        copy.start()
    return copies


def add_embedding(state_ref, index_ref, table, kinds, features, write):
    tokens = index_ref.shape[0]
    group = table.shape[0] // kinds
    spread_tokens = (iota((tokens, tokens * kinds), 1) // kinds == iota((tokens, tokens * kinds), 0)).astype(BF16)
    wide = lax.dot_general(
        index_ref[...].astype(F32).astype(BF16), spread_tokens, TN, preferred_element_type=F32
    )
    onehot = (wide == (iota(wide.shape, 1) % kinds).astype(F32)).astype(BF16)
    width = group * features
    for n in range(tokens // group):
        rows = dot(onehot[:, n * group * kinds : (n + 1) * group * kinds], table)
        write(n * width, (state_ref[:, n * width : (n + 1) * width].astype(F32) + rows).astype(BF16))


def embed_own_kernel(
    state_hbm, index_hbm, table_hbm, out_ref, wide_ref, state_ref, index_ref, table_ref, sems
):
    copies = fetch((index_hbm, table_hbm, state_hbm), (index_ref, table_ref, state_ref), sems)
    kinds, features = table_ref.shape
    copies[1].wait()
    wide_ref[...] = spread(
        wide_ref.shape[0],
        lambda r: r % kinds,
        table_ref[...],
        wide_ref.shape[1],
        lambda c: c % features,
        lambda r, c: r // kinds == c // features,
    )
    copies[0].wait()
    copies[2].wait()

    def write(at, value):
        out_ref[:, at : at + value.shape[1]] = value

    add_embedding(state_ref, index_ref, wide_ref[...], kinds, features, write)


def embed_group_kernel(kinds, size, own_ref, wide_ref, *refs):
    states, indices, out_ref = refs[: size - 1], refs[size - 1 : 2 * size - 2], refs[2 * size - 2]
    width = own_ref.shape[1]
    position = lax.rem(lax.axis_index("col"), size)
    out_ref[:, pl.ds(pl.multiple_of(position * width, width), width)] = own_ref[...]
    for n, (state, index) in enumerate(zip(states, indices, strict=True)):
        first = lax.rem(position + n + 1, size) * width

        def write(at, value, first=first):
            out_ref[:, pl.ds(pl.multiple_of(first + at, value.shape[1]), value.shape[1])] = value

        add_embedding(state, index, wide_ref[...], kinds, width // index.shape[0], write)


def weights_kernel(
    kinds_hbm,
    first_hbm,
    second_hbm,
    outer_hbm,
    bias_hbm,
    mask_hbm,
    pair_hbm,
    gate_up_hbm,
    down_hbm,
    left_hbm,
    right_hbm,
    gain_hbm,
    distance_hbm,
    last_hbm,
    embedded_ref,
    first_out,
    mask_out,
    base_out,
    outer_out,
    pair_out,
    gate_up_out,
    down_out,
    gain_out,
    left_out,
    right_out,
    distance_out,
    last_out,
    tiles_out,
    kinds_ref,
    first_ref,
    second_ref,
    outer_ref,
    bias_ref,
    mask_ref,
    left_ref,
    right_ref,
    distance_ref,
    last_ref,
    wide,
    rows,
    sems,
):
    copies = fetch(
        (left_hbm, right_hbm, kinds_hbm, first_hbm, second_hbm, bias_hbm, mask_hbm, distance_hbm, last_hbm)
        + (outer_hbm, pair_hbm, gate_up_hbm, down_hbm, gain_hbm),
        (left_ref, right_ref, kinds_ref, first_ref, second_ref, bias_ref, mask_ref, distance_ref, last_ref)
        + (outer_ref, pair_out, gate_up_out, down_out, gain_out),
        sems,
    )
    channels = outer_ref.shape[1]
    length = first_out.shape[0]
    side = left_hbm.shape[1]
    steps = outer_ref.shape[0] // side
    for copy in copies[:9]:
        copy.wait()
    features, c_width = left_ref.shape
    lanes = 4 * c_width
    left_out[...] = spread(
        8 * features,
        lambda r: r % features,
        left_ref[...],
        4 * lanes,
        lambda c: c % c_width,
        lambda r, c: r // features == 2 * (c // lanes) + c % (lanes // 2) // c_width,
    )
    project_left([(0, embedded_ref)], left_out, tiles_out)
    e_width = right_ref.shape[1]
    turned = lax.dot_general(
        (iota((8 * e_width, e_width), 0) // 8 == iota((8 * e_width, e_width), 1)).astype(BF16),
        right_ref[...],
        NT,
        preferred_element_type=F32,
    ).astype(BF16)
    repeat = (iota((features, 8 * features), 1) % features == iota((features, 8 * features), 0)).astype(BF16)
    shape = right_out.shape
    right_out[...] = jnp.where(
        iota(shape, 0) % 8 == iota(shape, 1) // features, dot(turned, repeat), 0.0
    ).astype(BF16)
    weight = distance_ref[...]
    none = jnp.zeros_like(weight)
    distance_out[...] = jnp.concatenate(
        [jnp.concatenate([weight, none], axis=1), jnp.concatenate([none, weight], axis=1)], axis=0
    )
    last_out[...] = jnp.concatenate([last_ref[...], last_ref[...]], axis=1)
    kinds = kinds_ref[...]
    onehot = (iota((first_ref.shape[0], kinds.shape[1]), 0) == kinds).astype(BF16)
    rows[...] = lax.dot_general(onehot, first_ref[...], TN, preferred_element_type=F32)
    first_out[...] = rows[pl.ds(pl.multiple_of(lax.axis_index("row") * length, length), length), :]
    rows[...] = lax.dot_general(onehot, second_ref[...], TN, preferred_element_type=F32)
    second = rows[pl.ds(pl.multiple_of(lax.axis_index("col") * length, length), length), :]
    blocks, columns = mask_ref.shape
    reach = (iota((length, columns), 0) // (length // columns) == iota((length, columns), 1)).astype(BF16)
    mask = lax.dot_general(
        reach, mask_ref[...].astype(F32).astype(BF16), NT, preferred_element_type=F32
    )
    bias = bias_ref[...].astype(F32)
    for b in range(blocks):
        part = jnp.broadcast_to(mask[:, b : b + 1], (length, channels))
        mask_out[b] = part
        base_out[b] = second + part * bias
    copies[9].wait()
    wide[...] = outer_ref[...].astype(F32)
    zero = jnp.zeros((side, channels), BF16)
    for e in range(steps):
        part = wide[pl.ds(e, side, stride=steps), :].astype(BF16)
        outer_out[pl.ds(2 * e * side, side), :] = jnp.concatenate([part, zero], axis=1)
        outer_out[pl.ds((2 * e + 1) * side, side), :] = jnp.concatenate([zero, part], axis=1)
    for copy in copies[10:]:
        copy.wait()


def project_left(parts, weight_ref, out_ref):
    group, columns = weight_ref.shape
    depth, width = parts[0][1].shape
    lanes = columns // 4
    half = iota((depth, columns), 1) % lanes < lanes // 2
    for k, part in parts:
        first = half_of("col", k, width // group * columns)
        for t in range(width // group):
            both = dot(part[:, t * group : (t + 1) * group], weight_ref[...])
            at = pl.ds(pl.multiple_of(first + t * columns, columns), columns)
            out_ref[0:depth, at] = jnp.where(half, both, 0.0).astype(BF16)
            out_ref[depth : 2 * depth, at] = jnp.where(half, 0.0, both).astype(BF16)


def project_right(part_ref, weight_ref, out_ref):
    depth, width = part_ref.shape
    group = weight_ref.shape[1]
    tokens = width // group * 8
    low = iota((8, 2 * depth), 1) < depth
    for t in range(0, tokens // 8, 2):
        sides = []
        for u in (t, t + 1):
            part = part_ref[:, u * group : (u + 1) * group]
            twice = jnp.concatenate([part, part], axis=0)
            sides.append(lax.dot_general(weight_ref[...], twice, NT, preferred_element_type=F32))
        for g in range(weight_ref.shape[0] // 16):
            rows = [
                jnp.where(low, s[16 * g : 16 * g + 8], s[16 * g + 8 : 16 * g + 16]) for s in sides
            ]
            out_ref[pl.ds(g * tokens + t * 8, 16), :] = jnp.concatenate(rows, axis=0).astype(BF16)


def project_left_kernel(other_ref, weight_ref, left_in, left_out):
    del left_in
    project_left([(1, other_ref)], weight_ref, left_out)


def project_right_kernel(right_ref, right_weight_ref, *rest):
    right_out = rest[-1]
    project_right(right_ref, right_weight_ref, right_out)


def half_of(axis, k, size):
    return pl.multiple_of(lax.rem(lax.axis_index(axis) // (lax.axis_size(axis) // 2) + k, 2) * size, size)


def pair_kernel(
    k,
    left_ref,
    right_ref,
    pair_ref,
    first_ref,
    mask_ref,
    base_ref,
    gain_ref,
    outer_ref,
    gate_up_ref,
    down_ref,
    distance_ref,
    *rest,
):
    pair_out, dist_out, outer, start = rest[-4:]
    length, size, channels = pair_out.shape
    block_rows = length // mask_ref.shape[0]
    second = pl.ds(half_of("row", k, size), size)
    pairs = length // 2
    depth, lanes = right_ref.shape[1] // 2, right_ref.shape[1]
    groups = right_ref.shape[0] // size
    step = min(groups, 256 // size)
    hid = down_ref.shape[0]
    bins = distance_ref.shape[0] // 2
    for p in range(0, pairs, 2):
        weight = left_ref[:, p * lanes : (p + 2) * lanes]
        for g in range(0, groups, step):
            got = dot(right_ref[g * size : (g + step) * size, :], weight).astype(BF16)
            for q in range(2):
                for h in range(step):
                    outer[(p + q) * size : (p + q + 1) * size, (g + h) * lanes : (g + h + 1) * lanes] = got[
                        h * size : (h + 1) * size, q * lanes : (q + 1) * lanes
                    ]
    part_rows = max(size, outer.shape[0] // 8)
    update = [
        dot(outer[n : n + part_rows], outer_ref[...]) for n in range(0, outer.shape[0], part_rows)
    ]
    for p in range(pairs):
        block = 2 * p // block_rows
        mask = mask_ref[block, second, :] * (1.0 / depth)
        base = base_ref[block, second, :]
        at = p * size % part_rows
        part = update[p * size // part_rows][at : at + size]
        for q in range(2):
            i = 2 * p + q
            start[q, p * size : (p + 1) * size, :] = (
                pair_ref[i, second, :].astype(F32)
                + (first_ref[i : i + 1, :] + base)
                + mask * part[:, q * channels : (q + 1) * channels]
            )
    half = min(start.shape[1], 512)
    for q, at in ((q, slice(n, n + half)) for q in range(2) for n in range(0, start.shape[1], half)):
        value = start[q, at]
        mean = jnp.mean(value, axis=-1, keepdims=True)
        centered = value - mean
        variance = jnp.mean(centered * centered, axis=-1, keepdims=True)
        normed = (centered * lax.rsqrt(variance + EPSILON) * gain_ref[...]).astype(BF16)
        gate_up = dot(normed, gate_up_ref[...])
        gate, up = gate_up[:, :hid], gate_up[:, hid:]
        hidden = (0.5 * gate * (1.0 + jnp.tanh(0.5 * gate)) * up).astype(BF16)
        start[q, at] = value + dot(hidden, down_ref[...])
    result = [start[q].astype(BF16) for q in range(2)]
    for p in range(pairs):
        for q in range(2):
            pair_out[2 * p + q] = result[q][p * size : (p + 1) * size]
    dist = lax.dot_general(
        jnp.concatenate(result, axis=1), distance_ref[...], NT, preferred_element_type=F32
    ).astype(BF16)
    for p in range(pairs):
        dist_out[:, 2 * p * bins : 2 * (p + 1) * bins] = dist[p * size : (p + 1) * size]


def own_kernel(order, *refs):
    count = len(order)
    parts, dists = refs[:count], refs[count : 2 * count]
    pair_out, own_ref, sems = refs[2 * count :]
    length, size, _ = parts[0].shape
    firsts = [half_of("row", k, size) for k in order]
    copies = fetch(parts, [pair_out.at[:, pl.ds(first, size)] for first in firsts], sems)
    pairs = length // 2
    lanes = dists[0].shape[1] // pairs
    low = iota((pairs, lanes), 1) < lanes // 2
    for k, dist in zip(order, dists, strict=True):
        first = half_of("row", k, size // 2)
        tiles = jnp.stack([dist[:, p * lanes : (p + 1) * lanes].astype(F32) for p in range(pairs)])
        turned = jnp.swapaxes(tiles, 0, 1)
        for j in range(0, size, 2):
            one, two = turned[j], turned[j + 1]
            own_ref[first + j // 2, pl.ds(0, pairs, stride=2), :] = jnp.where(
                low, one, pltpu.roll(two, lanes // 2, 1)
            )
            own_ref[first + j // 2, pl.ds(1, pairs, stride=2), :] = jnp.where(
                low, pltpu.roll(one, lanes // 2, 1), two
            )
    for copy in copies:
        copy.wait()


def final_kernel(order, own_ref, bias_ref, *refs):
    out_ref = refs[len(order)]
    lanes = bias_ref.shape[1]

    def write(swapped):
        for k, part in zip(order, refs, strict=False):
            size, width = part.shape
            first = (k + swapped) % 2 * size
            rows = slice(first, first + size)
            for t in range(width // lanes):
                at = slice(t * lanes, (t + 1) * lanes)
                value = own_ref[t, rows, :] + part[:, at].astype(F32) + bias_ref[...]
                out_ref[rows, at] = value.astype(BF16)

    half = lax.axis_index("col") // (lax.axis_size("col") // 2)
    pl.when(half == 0)(functools.partial(write, 0))
    pl.when(half == 1)(functools.partial(write, 1))


PAIR_COST = pl.CostEstimate(flops=5_000_000_000, bytes_accessed=16_000_000, transcendentals=0)
COST = pl.CostEstimate(flops=0, bytes_accessed=0, transcendentals=0)


def params(mib):
    return pltpu.CompilerParams(vmem_limit_bytes=mib * MIB)


def in_hbm(*arrays):
    return [pltpu.with_memory_space_constraint(a, pltpu.HBM) for a in arrays]


VMEM = pl.BlockSpec(memory_space=pltpu.VMEM)
HBM = pl.BlockSpec(memory_space=pltpu.HBM)


def local(
    row_count,
    col_count,
    pair_state,
    token_kinds,
    first_type_table,
    second_type_table,
    alignment_state,
    alignment_index,
    alignment_table,
    first_weight,
    second_weight,
    outer_product_weight,
    outer_product_bias,
    pair_block_mask,
    transition_gain,
    transition_gate_up,
    transition_down,
    distance_weight,
    distance_bias,
):
    length = pair_state.shape[0]
    channels = pair_state.shape[2]
    depth = alignment_index.shape[0]
    features, c_width = first_weight.shape
    e_width = second_weight.shape[1]
    bins = distance_weight.shape[1]
    axes = ("row", "col")
    size = col_count // 2

    def moved(value, target):
        pairs = [
            (r * col_count + c, target(r, c)[0] * col_count + target(r, c)[1])
            for r in range(row_count)
            for c in range(col_count)
        ]
        return lax.ppermute(value, axes, pairs)

    def neighbour(value, k):
        return moved(value, lambda r, c: (r, c - c % size + (c - k) % size))

    turned_index = alignment_index.T
    other_indices = [neighbour(turned_index, k) for k in range(1, size)]
    other_states = [neighbour(alignment_state, k) for k in range(1, size)]
    kinds = alignment_table.shape[0]
    group = min(alignment_index.shape[1], 256 // features)
    own_embedded, wide_table = pl.pallas_call(
        embed_own_kernel,
        out_shape=(
            jax.ShapeDtypeStruct(alignment_state.shape, BF16),
            jax.ShapeDtypeStruct((group * kinds, group * features), BF16),
        ),
        in_specs=[HBM] * 3,
        out_specs=(VMEM,) * 2,
        scratch_shapes=[
            pltpu.VMEM(alignment_state.shape, BF16),
            pltpu.VMEM(turned_index.shape, jnp.int32),
            pltpu.VMEM(alignment_table.shape, BF16),
            pltpu.SemaphoreType.DMA((3,)),
        ],
        compiler_params=params(4),
        cost_estimate=COST,
        name="embed_own",
    )(*in_hbm(alignment_state, turned_index, alignment_table))
    embedded = pl.pallas_call(
        functools.partial(embed_group_kernel, kinds, size),
        out_shape=jax.ShapeDtypeStruct((depth, size * alignment_state.shape[1]), BF16),
        in_specs=[VMEM] * (2 * size),
        out_specs=VMEM,
        compiler_params=params(4),
        cost_estimate=COST,
        name="embed_group",
    )(own_embedded, wide_table, *other_states, *other_indices)

    rights = {
        k: moved(embedded, lambda r, c, k=k: ((c - size * k) % row_count, r)) for k in ORDER
    }
    other = moved(embedded, lambda r, c: (r, (c + size) % col_count))

    blocks = pair_block_mask.shape[0]
    maps = jax.ShapeDtypeStruct((blocks, length, channels), F32)
    left_shape = jax.ShapeDtypeStruct((2 * depth, 2 * length * c_width), BF16)
    (
        first_rows,
        masks,
        bases,
        outer_weight,
        pair_in,
        gate_up,
        down,
        gain,
        left_weight,
        right_weight,
        turned_distance,
        last,
        left_tiles,
    ) = pl.pallas_call(
        weights_kernel,
        out_shape=(
            jax.ShapeDtypeStruct((length, channels), F32),
            maps,
            maps,
            jax.ShapeDtypeStruct((2 * c_width * e_width, 2 * channels), BF16),
            jax.ShapeDtypeStruct(pair_state.shape, BF16),
            jax.ShapeDtypeStruct(transition_gate_up.shape, BF16),
            jax.ShapeDtypeStruct(transition_down.shape, BF16),
            jax.ShapeDtypeStruct((1, channels), F32),
            jax.ShapeDtypeStruct((8 * features, 16 * c_width), BF16),
            jax.ShapeDtypeStruct((8 * e_width, 8 * features), BF16),
            jax.ShapeDtypeStruct((2 * bins, 2 * channels), BF16),
            jax.ShapeDtypeStruct((1, 2 * bins), F32),
            left_shape,
        ),
        in_specs=[HBM] * 14 + [VMEM],
        out_specs=(VMEM,) * 13,
        scratch_shapes=[
            pltpu.VMEM((1, token_kinds.shape[0]), jnp.int32),
            pltpu.VMEM(first_type_table.shape, BF16),
            pltpu.VMEM(second_type_table.shape, BF16),
            pltpu.VMEM(outer_product_weight.shape, BF16),
            pltpu.VMEM((1, channels), BF16),
            pltpu.VMEM(pair_block_mask.shape, jnp.int32),
            pltpu.VMEM(first_weight.shape, BF16),
            pltpu.VMEM(second_weight.shape, BF16),
            pltpu.VMEM((bins, channels), BF16),
            pltpu.VMEM((1, bins), F32),
            pltpu.VMEM(outer_product_weight.shape, F32),
            pltpu.VMEM((token_kinds.shape[0], channels), F32),
            pltpu.SemaphoreType.DMA((14,)),
        ],
        compiler_params=params(8),
        cost_estimate=COST,
        name="weights",
    )(
        *in_hbm(
            token_kinds.reshape(1, -1),
            first_type_table,
            second_type_table,
            outer_product_weight,
            outer_product_bias.reshape(1, -1),
            pair_block_mask,
            pair_state,
            transition_gate_up,
            transition_down,
            first_weight,
            second_weight,
            transition_gain.reshape(1, -1),
            distance_weight.T,
            distance_bias.reshape(1, -1),
        ),
        embedded,
    )

    half = length // 2
    right_shape = jax.ShapeDtypeStruct((e_width // 2 * half, 2 * depth), BF16)
    pair_parts, dist_parts, mirror_parts = [], [], []
    left_tiles = pl.pallas_call(
        project_left_kernel,
        out_shape=left_shape,
        in_specs=[VMEM] * 3,
        out_specs=VMEM,
        input_output_aliases={2: 0},
        compiler_params=params(4),
        cost_estimate=COST,
        name="project_left",
    )(other, left_weight, left_tiles)
    for n, k in enumerate(ORDER):
        after = [left_tiles] if n == 0 else []
        right_tiles = pl.pallas_call(
            project_right_kernel,
            out_shape=right_shape,
            in_specs=[VMEM] * (2 + len(after)),
            out_specs=VMEM,
            compiler_params=params(4),
            cost_estimate=COST,
            name="project_right",
        )(rights[k], right_weight, *after)
        before = dist_parts[-1:]
        pair_part, dist_part = pl.pallas_call(
            functools.partial(pair_kernel, k),
            out_shape=(
                jax.ShapeDtypeStruct((length, half, channels), BF16),
                jax.ShapeDtypeStruct((half, length * bins), BF16),
            ),
            in_specs=[VMEM] * (11 + len(before)),
            out_specs=(VMEM,) * 2,
            scratch_shapes=[
                pltpu.VMEM((length // 2 * half, 2 * c_width * e_width), BF16),
                pltpu.VMEM((2, length // 2 * half, channels), F32),
            ],
            compiler_params=params(24),
            cost_estimate=PAIR_COST,
            name="pairs",
        )(
            left_tiles,
            right_tiles,
            pair_in,
            first_rows,
            masks,
            bases,
            gain,
            outer_weight,
            gate_up,
            down,
            turned_distance,
            *before,
        )
        pair_parts.append(pair_part)
        dist_parts.append(dist_part)
        if n == 0:
            crossed = moved(dist_part, lambda r, c: (r, (c + size) % col_count))
            mirror_parts.append(moved(crossed, lambda r, c: ((c + size) % col_count, r)))
        else:
            mirror_parts.append(moved(dist_part, lambda r, c: (c, r)))
    pair_out, own = pl.pallas_call(
        functools.partial(own_kernel, ORDER),
        out_shape=(
            jax.ShapeDtypeStruct(pair_state.shape, BF16),
            jax.ShapeDtypeStruct((length // 2, length, 2 * bins), F32),
        ),
        in_specs=[VMEM] * (2 * len(pair_parts)),
        out_specs=(HBM, VMEM),
        scratch_shapes=[pltpu.SemaphoreType.DMA((len(pair_parts),))],
        compiler_params=params(8),
        cost_estimate=COST,
        name="own",
    )(*pair_parts, *dist_parts)
    distogram = pl.pallas_call(
        functools.partial(final_kernel, ORDER),
        out_shape=jax.ShapeDtypeStruct((length, length * bins), BF16),
        in_specs=[VMEM] * 4,
        out_specs=VMEM,
        compiler_params=params(4),
        cost_estimate=COST,
        name="final",
    )(own, last, *mirror_parts)
    return pair_out, distogram


def solution(mesh):
    split = P(("conf", "row"), "col")
    tokens = P(None, ("conf", "row", "col"))
    in_specs = (
        P(("conf", "row"), "col", None),
        P("conf"),
        P(),
        P(),
        tokens,
        tokens,
        P(),
        P(),
        P(),
        P(),
        P(),
        split,
        P(),
        P(),
        P(),
        P(),
        P(),
    )
    return jax.shard_map(
        functools.partial(local, mesh.shape["row"], mesh.shape["col"]),
        mesh=mesh,
        in_specs=in_specs,
        out_specs=(P(("conf", "row"), "col", None), split),
        check_vma=False,
    )
```

```python
import functools

import jax
import jax.numpy as jnp
from jax import lax
from jax.experimental import pallas as pl
from jax.experimental.pallas import tpu as pltpu
from jax.sharding import PartitionSpec as P

EPSILON = 1e-05
F32 = jnp.float32
BF16 = jnp.bfloat16
NT = (((1,), (1,)), ((), ()))
TN = (((0,), (0,)), ((), ()))
MIB = 1024 * 1024
PARTS = ((1, 0, 8), (0, 0, 6), (0, 6, 2))


def iota(shape, dim):
    return lax.broadcasted_iota(jnp.int32, shape, dim)


def dot(a, b):
    return jnp.dot(a, b, preferred_element_type=F32)


def spread(rows, row_key, weight, columns, column_key, keep):
    left = (row_key(iota((rows, weight.shape[0]), 0)) == iota((rows, weight.shape[0]), 1)).astype(BF16)
    right = (column_key(iota((weight.shape[1], columns), 1)) == iota((weight.shape[1], columns), 0)).astype(BF16)
    full = dot(dot(left, weight).astype(BF16), right)
    at = iota((rows, columns), 0), iota((rows, columns), 1)
    return jnp.where(keep(*at), full, 0.0).astype(BF16)


def fetch(sources, targets, sems):
    copies = [pltpu.make_async_copy(s, t, sems.at[n]) for n, (s, t) in enumerate(zip(sources, targets, strict=True))]
    for copy in copies:
        copy.start()
    return copies


def add_embedding(state_ref, index_ref, table, kinds, features, write):
    tokens = index_ref.shape[0]
    group = table.shape[0] // kinds
    spread_tokens = (iota((tokens, tokens * kinds), 1) // kinds == iota((tokens, tokens * kinds), 0)).astype(BF16)
    wide = lax.dot_general(
        index_ref[...].astype(F32).astype(BF16), spread_tokens, TN, preferred_element_type=F32
    )
    onehot = (wide == (iota(wide.shape, 1) % kinds).astype(F32)).astype(BF16)
    width = group * features
    for n in range(tokens // group):
        rows = dot(onehot[:, n * group * kinds : (n + 1) * group * kinds], table)
        write(n * width, (state_ref[:, n * width : (n + 1) * width].astype(F32) + rows).astype(BF16))


def embed_own_kernel(
    state_hbm, index_hbm, table_hbm, out_ref, wide_ref, state_ref, index_ref, table_ref, sems
):
    copies = fetch((index_hbm, table_hbm, state_hbm), (index_ref, table_ref, state_ref), sems)
    kinds, features = table_ref.shape
    copies[1].wait()
    wide_ref[...] = spread(
        wide_ref.shape[0],
        lambda r: r % kinds,
        table_ref[...],
        wide_ref.shape[1],
        lambda c: c % features,
        lambda r, c: r // kinds == c // features,
    )
    copies[0].wait()
    copies[2].wait()

    def write(at, value):
        out_ref[:, at : at + value.shape[1]] = value

    add_embedding(state_ref, index_ref, wide_ref[...], kinds, features, write)


def embed_group_kernel(kinds, size, own_ref, wide_ref, *refs):
    states, indices, out_ref = refs[: size - 1], refs[size - 1 : 2 * size - 2], refs[2 * size - 2]
    width = own_ref.shape[1]
    position = lax.rem(lax.axis_index("col"), size)
    out_ref[:, pl.ds(pl.multiple_of(position * width, width), width)] = own_ref[...]
    for n, (state, index) in enumerate(zip(states, indices, strict=True)):
        first = lax.rem(position + n + 1, size) * width

        def write(at, value, first=first):
            out_ref[:, pl.ds(pl.multiple_of(first + at, value.shape[1]), value.shape[1])] = value

        add_embedding(state, index, wide_ref[...], kinds, width // index.shape[0], write)


def weights_kernel(
    kinds_hbm,
    first_hbm,
    second_hbm,
    outer_hbm,
    bias_hbm,
    mask_hbm,
    pair_hbm,
    gate_up_hbm,
    down_hbm,
    left_hbm,
    right_hbm,
    gain_hbm,
    distance_hbm,
    last_hbm,
    embedded_ref,
    first_out,
    mask_out,
    base_out,
    outer_out,
    pair_out,
    gate_up_out,
    down_out,
    gain_out,
    left_out,
    right_out,
    distance_out,
    last_out,
    tiles_out,
    kinds_ref,
    first_ref,
    second_ref,
    outer_ref,
    bias_ref,
    mask_ref,
    left_ref,
    right_ref,
    distance_ref,
    last_ref,
    wide,
    rows,
    sems,
):
    copies = fetch(
        (left_hbm, right_hbm, kinds_hbm, first_hbm, second_hbm, bias_hbm, mask_hbm, distance_hbm, last_hbm)
        + (outer_hbm, pair_hbm, gate_up_hbm, down_hbm, gain_hbm),
        (left_ref, right_ref, kinds_ref, first_ref, second_ref, bias_ref, mask_ref, distance_ref, last_ref)
        + (outer_ref, pair_out, gate_up_out, down_out, gain_out),
        sems,
    )
    channels = outer_ref.shape[1]
    length = first_out.shape[0]
    side = left_hbm.shape[1]
    steps = outer_ref.shape[0] // side
    for copy in copies[:9]:
        copy.wait()
    features, c_width = left_ref.shape
    lanes = 4 * c_width
    left_out[...] = spread(
        8 * features,
        lambda r: r % features,
        left_ref[...],
        4 * lanes,
        lambda c: c % c_width,
        lambda r, c: r // features == 2 * (c // lanes) + c % (lanes // 2) // c_width,
    )
    project_left([(0, embedded_ref)], left_out, tiles_out)
    e_width = right_ref.shape[1]
    turned = lax.dot_general(
        (iota((8 * e_width, e_width), 0) // 8 == iota((8 * e_width, e_width), 1)).astype(BF16),
        right_ref[...],
        NT,
        preferred_element_type=F32,
    ).astype(BF16)
    repeat = (iota((features, 8 * features), 1) % features == iota((features, 8 * features), 0)).astype(BF16)
    shape = right_out.shape
    right_out[...] = jnp.where(
        iota(shape, 0) % 8 == iota(shape, 1) // features, dot(turned, repeat), 0.0
    ).astype(BF16)
    weight = distance_ref[...]
    none = jnp.zeros_like(weight)
    distance_out[...] = jnp.concatenate(
        [jnp.concatenate([weight, none], axis=1), jnp.concatenate([none, weight], axis=1)], axis=0
    )
    last_out[...] = jnp.concatenate([last_ref[...], last_ref[...]], axis=1)
    kinds = kinds_ref[...]
    onehot = (iota((first_ref.shape[0], kinds.shape[1]), 0) == kinds).astype(BF16)
    rows[...] = lax.dot_general(onehot, first_ref[...], TN, preferred_element_type=F32)
    first_out[...] = rows[pl.ds(pl.multiple_of(lax.axis_index("row") * length, length), length), :]
    rows[...] = lax.dot_general(onehot, second_ref[...], TN, preferred_element_type=F32)
    second = rows[pl.ds(pl.multiple_of(lax.axis_index("col") * length, length), length), :]
    blocks, columns = mask_ref.shape
    reach = (iota((length, columns), 0) // (length // columns) == iota((length, columns), 1)).astype(BF16)
    mask = lax.dot_general(
        reach, mask_ref[...].astype(F32).astype(BF16), NT, preferred_element_type=F32
    )
    bias = bias_ref[...].astype(F32)
    for b in range(blocks):
        part = jnp.broadcast_to(mask[:, b : b + 1], (length, channels))
        mask_out[b] = part
        base_out[b] = second + part * bias
    copies[9].wait()
    wide[...] = outer_ref[...].astype(F32)
    zero = jnp.zeros((side, channels), BF16)
    for e in range(steps):
        part = wide[pl.ds(e, side, stride=steps), :].astype(BF16)
        outer_out[pl.ds(2 * e * side, side), :] = jnp.concatenate([part, zero], axis=1)
        outer_out[pl.ds((2 * e + 1) * side, side), :] = jnp.concatenate([zero, part], axis=1)
    for copy in copies[10:]:
        copy.wait()


def project_left(parts, weight_ref, out_ref):
    group, columns = weight_ref.shape
    depth, width = parts[0][1].shape
    lanes = columns // 4
    half = iota((depth, columns), 1) % lanes < lanes // 2
    for k, part in parts:
        first = half_of("col", k, width // group * columns)
        for t in range(width // group):
            both = dot(part[:, t * group : (t + 1) * group], weight_ref[...])
            at = pl.ds(pl.multiple_of(first + t * columns, columns), columns)
            out_ref[0:depth, at] = jnp.where(half, both, 0.0).astype(BF16)
            out_ref[depth : 2 * depth, at] = jnp.where(half, 0.0, both).astype(BF16)


def project_right(part_ref, weight_ref, out_ref):
    depth, width = part_ref.shape
    group = weight_ref.shape[1]
    tokens = width // group * 8
    low = iota((8, 2 * depth), 1) < depth
    for t in range(0, tokens // 8, 2):
        sides = []
        for u in (t, t + 1):
            part = part_ref[:, u * group : (u + 1) * group]
            twice = jnp.concatenate([part, part], axis=0)
            sides.append(lax.dot_general(weight_ref[...], twice, NT, preferred_element_type=F32))
        for g in range(weight_ref.shape[0] // 16):
            rows = [
                jnp.where(low, s[16 * g : 16 * g + 8], s[16 * g + 8 : 16 * g + 16]) for s in sides
            ]
            out_ref[pl.ds(g * tokens + t * 8, 16), :] = jnp.concatenate(rows, axis=0).astype(BF16)


def project_left_kernel(other_ref, weight_ref, left_in, left_out):
    del left_in
    project_left([(1, other_ref)], weight_ref, left_out)


def half_of(axis, k, size):
    return pl.multiple_of(lax.rem(lax.axis_index(axis) // (lax.axis_size(axis) // 2) + k, 2) * size, size)


def pair_kernel(
    part,
    left_ref,
    embedded_ref,
    right_weight_ref,
    pair_ref,
    first_ref,
    mask_ref,
    base_ref,
    gain_ref,
    outer_ref,
    gate_up_ref,
    down_ref,
    distance_ref,
    *rest,
):
    pair_out, dist_out, right_ref, outer, start = rest[-5:]
    project_right(embedded_ref, right_weight_ref, right_ref)
    rows, size, channels = pair_out.shape
    block_rows = pair_ref.shape[0] // mask_ref.shape[0]
    k, eighth, _ = part
    second = pl.ds(half_of("row", k, size), size)
    pairs = rows // 2
    first_pair = eighth * pair_ref.shape[0] // 16
    depth, lanes = right_ref.shape[1] // 2, right_ref.shape[1]
    groups = right_ref.shape[0] // size
    step = min(groups, 256 // size)
    hid = down_ref.shape[0]
    bins = distance_ref.shape[0] // 2
    for p in range(0, pairs, 2):
        weight = left_ref[:, (first_pair + p) * lanes : (first_pair + p + 2) * lanes]
        for g in range(0, groups, step):
            got = dot(right_ref[g * size : (g + step) * size, :], weight).astype(BF16)
            for q in range(2):
                for h in range(step):
                    outer[(p + q) * size : (p + q + 1) * size, (g + h) * lanes : (g + h + 1) * lanes] = got[
                        h * size : (h + 1) * size, q * lanes : (q + 1) * lanes
                    ]
    part_rows = max(128, outer.shape[0] // 8)
    update = [
        dot(outer[n : n + part_rows], outer_ref[...]) for n in range(0, outer.shape[0], part_rows)
    ]
    for p in range(pairs):
        block = 2 * (first_pair + p) // block_rows
        mask = mask_ref[block, second, :] * (1.0 / depth)
        base = base_ref[block, second, :]
        at = p * size % part_rows
        part = update[p * size // part_rows][at : at + size]
        for q in range(2):
            i = 2 * (first_pair + p) + q
            start[q, p * size : (p + 1) * size, :] = (
                pair_ref[i, second, :].astype(F32)
                + (first_ref[i : i + 1, :] + base)
                + mask * part[:, q * channels : (q + 1) * channels]
            )
    half = start.shape[1] if start.shape[1] < 1024 else 512
    for q, at in ((q, slice(n, n + half)) for q in range(2) for n in range(0, start.shape[1], half)):
        value = start[q, at]
        mean = jnp.mean(value, axis=-1, keepdims=True)
        centered = value - mean
        variance = jnp.mean(centered * centered, axis=-1, keepdims=True)
        normed = (centered * lax.rsqrt(variance + EPSILON) * gain_ref[...]).astype(BF16)
        gate_up = dot(normed, gate_up_ref[...])
        gate, up = gate_up[:, :hid], gate_up[:, hid:]
        hidden = (0.5 * gate * (1.0 + jnp.tanh(0.5 * gate)) * up).astype(BF16)
        start[q, at] = value + dot(hidden, down_ref[...])
    result = [start[q].astype(BF16) for q in range(2)]
    for p in range(pairs):
        for q in range(2):
            pair_out[2 * p + q] = result[q][p * size : (p + 1) * size]
    dist = lax.dot_general(
        jnp.concatenate(result, axis=1), distance_ref[...], NT, preferred_element_type=F32
    ).astype(BF16)
    for p in range(pairs):
        dist_out[:, 2 * p * bins : 2 * (p + 1) * bins] = dist[p * size : (p + 1) * size]


def own_kernel(*refs):
    count = len(PARTS)
    pairs_in, dists = refs[:count], refs[count : 2 * count]
    pair_out, own_ref, sems = refs[2 * count :]
    targets = []
    length = pair_out.shape[0]
    for (k, eighth, _), part in zip(PARTS, pairs_in, strict=True):
        rows, size, _ = part.shape
        targets.append(pair_out.at[pl.ds(eighth * length // 8, rows), pl.ds(half_of("row", k, size), size)])
    copies = fetch(pairs_in, targets, sems)
    lanes = own_ref.shape[2]
    for (k, eighth, _), part, dist in zip(PARTS, pairs_in, dists, strict=True):
        rows, size, _ = part.shape
        pairs = rows // 2
        above = eighth * length // 8
        low = iota((pairs, lanes), 1) < lanes // 2
        first = half_of("row", k, size // 2)
        tiles = jnp.stack([dist[:, p * lanes : (p + 1) * lanes].astype(F32) for p in range(pairs)])
        turned = jnp.swapaxes(tiles, 0, 1)
        for j in range(0, size, 2):
            one, two = turned[j], turned[j + 1]
            own_ref[first + j // 2, pl.ds(above, pairs, stride=2), :] = jnp.where(
                low, one, pltpu.roll(two, lanes // 2, 1)
            )
            own_ref[first + j // 2, pl.ds(above + 1, pairs, stride=2), :] = jnp.where(
                low, pltpu.roll(one, lanes // 2, 1), two
            )
    for copy in copies:
        copy.wait()


def final_kernel(own_ref, bias_ref, *refs):
    out_ref = refs[len(PARTS)]
    lanes = bias_ref.shape[1]

    def write(swapped):
        for (k, eighth, _), part in zip(PARTS, refs, strict=False):
            size, width = part.shape
            first = (k + swapped) % 2 * size
            rows = slice(first, first + size)
            for t in range(width // lanes):
                tile = eighth * out_ref.shape[1] // (8 * lanes) + t
                value = own_ref[tile, rows, :] + part[:, t * lanes : (t + 1) * lanes].astype(F32) + bias_ref[...]
                out_ref[rows, tile * lanes : (tile + 1) * lanes] = value.astype(BF16)

    half = lax.axis_index("col") // (lax.axis_size("col") // 2)
    pl.when(half == 0)(functools.partial(write, 0))
    pl.when(half == 1)(functools.partial(write, 1))


PAIR_COST = pl.CostEstimate(flops=5_000_000_000, bytes_accessed=16_000_000, transcendentals=0)
COST = pl.CostEstimate(flops=0, bytes_accessed=0, transcendentals=0)


def params(mib):
    return pltpu.CompilerParams(vmem_limit_bytes=mib * MIB)


def in_hbm(*arrays):
    return [pltpu.with_memory_space_constraint(a, pltpu.HBM) for a in arrays]


VMEM = pl.BlockSpec(memory_space=pltpu.VMEM)
HBM = pl.BlockSpec(memory_space=pltpu.HBM)


def local(
    row_count,
    col_count,
    pair_state,
    token_kinds,
    first_type_table,
    second_type_table,
    alignment_state,
    alignment_index,
    alignment_table,
    first_weight,
    second_weight,
    outer_product_weight,
    outer_product_bias,
    pair_block_mask,
    transition_gain,
    transition_gate_up,
    transition_down,
    distance_weight,
    distance_bias,
):
    length = pair_state.shape[0]
    channels = pair_state.shape[2]
    depth = alignment_index.shape[0]
    features, c_width = first_weight.shape
    e_width = second_weight.shape[1]
    bins = distance_weight.shape[1]
    axes = ("row", "col")
    size = col_count // 2

    def moved(value, target):
        pairs = [
            (r * col_count + c, target(r, c)[0] * col_count + target(r, c)[1])
            for r in range(row_count)
            for c in range(col_count)
        ]
        return lax.ppermute(value, axes, pairs)

    def neighbour(value, k):
        return moved(value, lambda r, c: (r, c - c % size + (c - k) % size))

    turned_index = alignment_index.T
    other_indices = [neighbour(turned_index, k) for k in range(1, size)]
    other_states = [neighbour(alignment_state, k) for k in range(1, size)]
    kinds = alignment_table.shape[0]
    group = min(alignment_index.shape[1], 256 // features)
    own_embedded, wide_table = pl.pallas_call(
        embed_own_kernel,
        out_shape=(
            jax.ShapeDtypeStruct(alignment_state.shape, BF16),
            jax.ShapeDtypeStruct((group * kinds, group * features), BF16),
        ),
        in_specs=[HBM] * 3,
        out_specs=(VMEM,) * 2,
        scratch_shapes=[
            pltpu.VMEM(alignment_state.shape, BF16),
            pltpu.VMEM(turned_index.shape, jnp.int32),
            pltpu.VMEM(alignment_table.shape, BF16),
            pltpu.SemaphoreType.DMA((3,)),
        ],
        compiler_params=params(4),
        cost_estimate=COST,
        name="embed_own",
    )(*in_hbm(alignment_state, turned_index, alignment_table))
    embedded = pl.pallas_call(
        functools.partial(embed_group_kernel, kinds, size),
        out_shape=jax.ShapeDtypeStruct((depth, size * alignment_state.shape[1]), BF16),
        in_specs=[VMEM] * (2 * size),
        out_specs=VMEM,
        compiler_params=params(4),
        cost_estimate=COST,
        name="embed_group",
    )(own_embedded, wide_table, *other_states, *other_indices)

    rights = {
        k: moved(embedded, lambda r, c, k=k: ((c - size * k) % row_count, r)) for k in (1, 0)
    }
    other = moved(embedded, lambda r, c: (r, (c + size) % col_count))

    blocks = pair_block_mask.shape[0]
    maps = jax.ShapeDtypeStruct((blocks, length, channels), F32)
    left_shape = jax.ShapeDtypeStruct((2 * depth, 2 * length * c_width), BF16)
    (
        first_rows,
        masks,
        bases,
        outer_weight,
        pair_in,
        gate_up,
        down,
        gain,
        left_weight,
        right_weight,
        turned_distance,
        last,
        left_tiles,
    ) = pl.pallas_call(
        weights_kernel,
        out_shape=(
            jax.ShapeDtypeStruct((length, channels), F32),
            maps,
            maps,
            jax.ShapeDtypeStruct((2 * c_width * e_width, 2 * channels), BF16),
            jax.ShapeDtypeStruct(pair_state.shape, BF16),
            jax.ShapeDtypeStruct(transition_gate_up.shape, BF16),
            jax.ShapeDtypeStruct(transition_down.shape, BF16),
            jax.ShapeDtypeStruct((1, channels), F32),
            jax.ShapeDtypeStruct((8 * features, 16 * c_width), BF16),
            jax.ShapeDtypeStruct((8 * e_width, 8 * features), BF16),
            jax.ShapeDtypeStruct((2 * bins, 2 * channels), BF16),
            jax.ShapeDtypeStruct((1, 2 * bins), F32),
            left_shape,
        ),
        in_specs=[HBM] * 14 + [VMEM],
        out_specs=(VMEM,) * 13,
        scratch_shapes=[
            pltpu.VMEM((1, token_kinds.shape[0]), jnp.int32),
            pltpu.VMEM(first_type_table.shape, BF16),
            pltpu.VMEM(second_type_table.shape, BF16),
            pltpu.VMEM(outer_product_weight.shape, BF16),
            pltpu.VMEM((1, channels), BF16),
            pltpu.VMEM(pair_block_mask.shape, jnp.int32),
            pltpu.VMEM(first_weight.shape, BF16),
            pltpu.VMEM(second_weight.shape, BF16),
            pltpu.VMEM((bins, channels), BF16),
            pltpu.VMEM((1, bins), F32),
            pltpu.VMEM(outer_product_weight.shape, F32),
            pltpu.VMEM((token_kinds.shape[0], channels), F32),
            pltpu.SemaphoreType.DMA((14,)),
        ],
        compiler_params=params(8),
        cost_estimate=COST,
        name="weights",
    )(
        *in_hbm(
            token_kinds.reshape(1, -1),
            first_type_table,
            second_type_table,
            outer_product_weight,
            outer_product_bias.reshape(1, -1),
            pair_block_mask,
            pair_state,
            transition_gate_up,
            transition_down,
            first_weight,
            second_weight,
            transition_gain.reshape(1, -1),
            distance_weight.T,
            distance_bias.reshape(1, -1),
        ),
        embedded,
    )

    half = length // 2
    pair_parts, dist_parts, mirror_parts = [], [], []
    left_tiles = pl.pallas_call(
        project_left_kernel,
        out_shape=left_shape,
        in_specs=[VMEM] * 3,
        out_specs=VMEM,
        input_output_aliases={2: 0},
        compiler_params=params(4),
        cost_estimate=COST,
        name="project_left",
    )(other, left_weight, left_tiles)
    for n, part in enumerate(PARTS):
        k, _, eighths = part
        rows = length * eighths // 8
        before = dist_parts[-1:]
        if n > 1:
            before = before + [crossed]
        pair_part, dist_part = pl.pallas_call(
            functools.partial(pair_kernel, part),
            out_shape=(
                jax.ShapeDtypeStruct((rows, half, channels), BF16),
                jax.ShapeDtypeStruct((half, rows * bins), BF16),
            ),
            in_specs=[VMEM] * (12 + len(before)),
            out_specs=(VMEM,) * 2,
            scratch_shapes=[
                pltpu.VMEM((e_width // 2 * half, 2 * depth), BF16),
                pltpu.VMEM((rows // 2 * half, 2 * c_width * e_width), BF16),
                pltpu.VMEM((2, rows // 2 * half, channels), F32),
            ],
            compiler_params=params(24),
            cost_estimate=PAIR_COST,
            name="pairs",
        )(
            left_tiles,
            rights[k],
            right_weight,
            pair_in,
            first_rows,
            masks,
            bases,
            gain,
            outer_weight,
            gate_up,
            down,
            turned_distance,
            *before,
        )
        pair_parts.append(pair_part)
        dist_parts.append(dist_part)
        if n == 0:
            crossed = moved(dist_part, lambda r, c: (r, (c + size) % col_count))
            mirror_parts.append(moved(crossed, lambda r, c: ((c + size) % col_count, r)))
        else:
            mirror_parts.append(moved(dist_part, lambda r, c: (c, r)))
    pair_out, own = pl.pallas_call(
        own_kernel,
        out_shape=(
            jax.ShapeDtypeStruct(pair_state.shape, BF16),
            jax.ShapeDtypeStruct((length // 2, length, 2 * bins), F32),
        ),
        in_specs=[VMEM] * (2 * len(pair_parts)),
        out_specs=(HBM, VMEM),
        scratch_shapes=[pltpu.SemaphoreType.DMA((len(pair_parts),))],
        compiler_params=params(8),
        cost_estimate=COST,
        name="own",
    )(*pair_parts, *dist_parts)
    distogram = pl.pallas_call(
        final_kernel,
        out_shape=jax.ShapeDtypeStruct((length, length * bins), BF16),
        in_specs=[VMEM] * (2 + len(mirror_parts)),
        out_specs=VMEM,
        compiler_params=params(4),
        cost_estimate=COST,
        name="final",
    )(own, last, *mirror_parts)
    return pair_out, distogram


def solution(mesh):
    split = P(("conf", "row"), "col")
    tokens = P(None, ("conf", "row", "col"))
    in_specs = (
        P(("conf", "row"), "col", None),
        P("conf"),
        P(),
        P(),
        tokens,
        tokens,
        P(),
        P(),
        P(),
        P(),
        P(),
        split,
        P(),
        P(),
        P(),
        P(),
        P(),
    )
    return jax.shard_map(
        functools.partial(local, mesh.shape["row"], mesh.shape["col"]),
        mesh=mesh,
        in_specs=in_specs,
        out_specs=(P(("conf", "row"), "col", None), split),
        check_vma=False,
    )
```

```python
import functools

import jax
import jax.numpy as jnp
from jax import lax
from jax.experimental import pallas as pl
from jax.experimental.pallas import tpu as pltpu
from jax.sharding import PartitionSpec as P

EPSILON = 1e-05
F32 = jnp.float32
BF16 = jnp.bfloat16
NT = (((1,), (1,)), ((), ()))
TN = (((0,), (0,)), ((), ()))
MIB = 1024 * 1024
PARTS = ((1, 0, 8), (0, 0, 6), (0, 6, 2))


def iota(shape, dim):
    return lax.broadcasted_iota(jnp.int32, shape, dim)


def dot(a, b):
    return jnp.dot(a, b, preferred_element_type=F32)


def spread(rows, row_key, weight, columns, column_key, keep):
    left = (row_key(iota((rows, weight.shape[0]), 0)) == iota((rows, weight.shape[0]), 1)).astype(BF16)
    right = (column_key(iota((weight.shape[1], columns), 1)) == iota((weight.shape[1], columns), 0)).astype(BF16)
    full = dot(dot(left, weight).astype(BF16), right)
    at = iota((rows, columns), 0), iota((rows, columns), 1)
    return jnp.where(keep(*at), full, 0.0).astype(BF16)


def fetch(sources, targets, sems):
    copies = [pltpu.make_async_copy(s, t, sems.at[n]) for n, (s, t) in enumerate(zip(sources, targets, strict=True))]
    for copy in copies:
        copy.start()
    return copies


def add_embedding(state_ref, index_ref, table, kinds, features, write):
    tokens = index_ref.shape[0]
    group = table.shape[0] // kinds
    spread_tokens = (iota((tokens, tokens * kinds), 1) // kinds == iota((tokens, tokens * kinds), 0)).astype(BF16)
    wide = lax.dot_general(
        index_ref[...].astype(F32).astype(BF16), spread_tokens, TN, preferred_element_type=F32
    )
    onehot = (wide == (iota(wide.shape, 1) % kinds).astype(F32)).astype(BF16)
    width = group * features
    for n in range(tokens // group):
        rows = dot(onehot[:, n * group * kinds : (n + 1) * group * kinds], table)
        write(n * width, (state_ref[:, n * width : (n + 1) * width].astype(F32) + rows).astype(BF16))


def embed_own_kernel(
    state_hbm, index_hbm, table_hbm, out_ref, wide_ref, state_ref, index_ref, table_ref, sems
):
    copies = fetch((index_hbm, table_hbm, state_hbm), (index_ref, table_ref, state_ref), sems)
    kinds, features = table_ref.shape
    copies[1].wait()
    wide_ref[...] = spread(
        wide_ref.shape[0],
        lambda r: r % kinds,
        table_ref[...],
        wide_ref.shape[1],
        lambda c: c % features,
        lambda r, c: r // kinds == c // features,
    )
    copies[0].wait()
    copies[2].wait()

    def write(at, value):
        out_ref[:, at : at + value.shape[1]] = value

    add_embedding(state_ref, index_ref, wide_ref[...], kinds, features, write)


def embed_group_kernel(kinds, size, own_ref, wide_ref, *refs):
    states, indices, out_ref = refs[: size - 1], refs[size - 1 : 2 * size - 2], refs[2 * size - 2]
    width = own_ref.shape[1]
    position = lax.rem(lax.axis_index("col"), size)
    out_ref[:, pl.ds(pl.multiple_of(position * width, width), width)] = own_ref[...]
    for n, (state, index) in enumerate(zip(states, indices, strict=True)):
        first = lax.rem(position + n + 1, size) * width

        def write(at, value, first=first):
            out_ref[:, pl.ds(pl.multiple_of(first + at, value.shape[1]), value.shape[1])] = value

        add_embedding(state, index, wide_ref[...], kinds, width // index.shape[0], write)


def weights_kernel(
    kinds_hbm,
    first_hbm,
    second_hbm,
    outer_hbm,
    bias_hbm,
    mask_hbm,
    pair_hbm,
    gate_up_hbm,
    down_hbm,
    left_hbm,
    right_hbm,
    gain_hbm,
    distance_hbm,
    last_hbm,
    embedded_ref,
    first_out,
    mask_out,
    base_out,
    outer_out,
    pair_out,
    gate_up_out,
    down_out,
    gain_out,
    left_out,
    right_out,
    distance_out,
    last_out,
    tiles_out,
    kinds_ref,
    first_ref,
    second_ref,
    outer_ref,
    bias_ref,
    mask_ref,
    left_ref,
    right_ref,
    distance_ref,
    last_ref,
    wide,
    rows,
    sems,
):
    copies = fetch(
        (left_hbm, right_hbm, kinds_hbm, first_hbm, second_hbm, bias_hbm, mask_hbm, distance_hbm, last_hbm)
        + (outer_hbm, pair_hbm, gate_up_hbm, down_hbm, gain_hbm),
        (left_ref, right_ref, kinds_ref, first_ref, second_ref, bias_ref, mask_ref, distance_ref, last_ref)
        + (outer_ref, pair_out, gate_up_out, down_out, gain_out),
        sems,
    )
    channels = outer_ref.shape[1]
    length = first_out.shape[0]
    side = left_hbm.shape[1]
    steps = outer_ref.shape[0] // side
    for copy in copies[:9]:
        copy.wait()
    features, c_width = left_ref.shape
    lanes = 4 * c_width
    left_out[...] = spread(
        8 * features,
        lambda r: r % features,
        left_ref[...],
        4 * lanes,
        lambda c: c % c_width,
        lambda r, c: r // features == 2 * (c // lanes) + c % (lanes // 2) // c_width,
    )
    project_left([(0, embedded_ref)], left_out, tiles_out)
    e_width = right_ref.shape[1]
    turned = lax.dot_general(
        (iota((8 * e_width, e_width), 0) // 8 == iota((8 * e_width, e_width), 1)).astype(BF16),
        right_ref[...],
        NT,
        preferred_element_type=F32,
    ).astype(BF16)
    repeat = (iota((features, 8 * features), 1) % features == iota((features, 8 * features), 0)).astype(BF16)
    shape = right_out.shape
    right_out[...] = jnp.where(
        iota(shape, 0) % 8 == iota(shape, 1) // features, dot(turned, repeat), 0.0
    ).astype(BF16)
    weight = distance_ref[...]
    none = jnp.zeros_like(weight)
    distance_out[...] = jnp.concatenate(
        [jnp.concatenate([weight, none], axis=1), jnp.concatenate([none, weight], axis=1)], axis=0
    )
    last_out[...] = jnp.concatenate([last_ref[...], last_ref[...]], axis=1)
    kinds = kinds_ref[...]
    onehot = (iota((first_ref.shape[0], kinds.shape[1]), 0) == kinds).astype(BF16)
    rows[...] = lax.dot_general(onehot, first_ref[...], TN, preferred_element_type=F32)
    first_out[...] = rows[pl.ds(pl.multiple_of(lax.axis_index("row") * length, length), length), :]
    rows[...] = lax.dot_general(onehot, second_ref[...], TN, preferred_element_type=F32)
    second = rows[pl.ds(pl.multiple_of(lax.axis_index("col") * length, length), length), :]
    blocks, columns = mask_ref.shape
    reach = (iota((length, columns), 0) // (length // columns) == iota((length, columns), 1)).astype(BF16)
    mask = lax.dot_general(
        reach, mask_ref[...].astype(F32).astype(BF16), NT, preferred_element_type=F32
    )
    bias = bias_ref[...].astype(F32)
    for b in range(blocks):
        part = jnp.broadcast_to(mask[:, b : b + 1], (length, channels))
        mask_out[b] = part
        base_out[b] = second + part * bias
    copies[9].wait()
    wide[...] = outer_ref[...].astype(F32)
    zero = jnp.zeros((side, channels), BF16)
    for e in range(steps):
        part = wide[pl.ds(e, side, stride=steps), :].astype(BF16)
        outer_out[pl.ds(2 * e * side, side), :] = jnp.concatenate([part, zero], axis=1)
        outer_out[pl.ds((2 * e + 1) * side, side), :] = jnp.concatenate([zero, part], axis=1)
    for copy in copies[10:]:
        copy.wait()


def project_left(parts, weight_ref, out_ref):
    group, columns = weight_ref.shape
    depth, width = parts[0][1].shape
    lanes = columns // 4
    half = iota((depth, columns), 1) % lanes < lanes // 2
    for k, part in parts:
        first = half_of("col", k, width // group * columns)
        for t in range(width // group):
            both = dot(part[:, t * group : (t + 1) * group], weight_ref[...])
            at = pl.ds(pl.multiple_of(first + t * columns, columns), columns)
            out_ref[0:depth, at] = jnp.where(half, both, 0.0).astype(BF16)
            out_ref[depth : 2 * depth, at] = jnp.where(half, 0.0, both).astype(BF16)


def project_right(part_ref, weight_ref, out_ref):
    depth, width = part_ref.shape
    group = weight_ref.shape[1]
    tokens = width // group * 8
    low = iota((8, 2 * depth), 1) < depth
    for t in range(0, tokens // 8, 2):
        sides = []
        for u in (t, t + 1):
            part = part_ref[:, u * group : (u + 1) * group]
            twice = jnp.concatenate([part, part], axis=0)
            sides.append(lax.dot_general(weight_ref[...], twice, NT, preferred_element_type=F32))
        for g in range(weight_ref.shape[0] // 16):
            rows = [
                jnp.where(low, s[16 * g : 16 * g + 8], s[16 * g + 8 : 16 * g + 16]) for s in sides
            ]
            out_ref[pl.ds(g * tokens + t * 8, 16), :] = jnp.concatenate(rows, axis=0).astype(BF16)


def project_left_kernel(other_ref, weight_ref, left_in, left_out):
    del left_in
    project_left([(1, other_ref)], weight_ref, left_out)


def half_of(axis, k, size):
    return pl.multiple_of(lax.rem(lax.axis_index(axis) // (lax.axis_size(axis) // 2) + k, 2) * size, size)


def pair_kernel(
    part,
    left_ref,
    embedded_ref,
    right_weight_ref,
    pair_ref,
    first_ref,
    mask_ref,
    base_ref,
    gain_ref,
    outer_ref,
    gate_up_ref,
    down_ref,
    distance_ref,
    *rest,
):
    pair_out, dist_out, right_ref, outer, start = rest[-5:]
    project_right(embedded_ref, right_weight_ref, right_ref)
    rows, size, channels = pair_out.shape
    block_rows = pair_ref.shape[0] // mask_ref.shape[0]
    k, eighth, _ = part
    second = pl.ds(half_of("row", k, size), size)
    pairs = rows // 2
    first_pair = eighth * pair_ref.shape[0] // 16
    depth, lanes = right_ref.shape[1] // 2, right_ref.shape[1]
    groups = right_ref.shape[0] // size
    step = min(groups, 256 // size)
    hid = down_ref.shape[0]
    bins = distance_ref.shape[0] // 2
    for p in range(0, pairs, 2):
        weight = left_ref[:, (first_pair + p) * lanes : (first_pair + p + 2) * lanes]
        for g in range(0, groups, step):
            got = dot(right_ref[g * size : (g + step) * size, :], weight).astype(BF16)
            for q in range(2):
                for h in range(step):
                    outer[(p + q) * size : (p + q + 1) * size, (g + h) * lanes : (g + h + 1) * lanes] = got[
                        h * size : (h + 1) * size, q * lanes : (q + 1) * lanes
                    ]
    part_rows = max(128, outer.shape[0] // 8)
    update = [
        dot(outer[n : n + part_rows], outer_ref[...]) for n in range(0, outer.shape[0], part_rows)
    ]
    for p in range(pairs):
        block = 2 * (first_pair + p) // block_rows
        mask = mask_ref[block, second, :] * (1.0 / depth)
        base = base_ref[block, second, :]
        at = p * size % part_rows
        part = update[p * size // part_rows][at : at + size]
        for q in range(2):
            i = 2 * (first_pair + p) + q
            start[q, p * size : (p + 1) * size, :] = (
                pair_ref[i, second, :].astype(F32)
                + (first_ref[i : i + 1, :] + base)
                + mask * part[:, q * channels : (q + 1) * channels]
            )
    count = start.shape[1]
    if count <= 256:
        blocks = [[(0, slice(0, count)), (1, slice(0, count))]]
    else:
        step = count // pl.cdiv(count, 512)
        blocks = [[(q, slice(n, n + step))] for q in range(2) for n in range(0, count, step)]
    for block in blocks:
        value = jnp.concatenate([start[q, at] for q, at in block], axis=0)
        mean = jnp.mean(value, axis=-1, keepdims=True)
        centered = value - mean
        variance = jnp.mean(centered * centered, axis=-1, keepdims=True)
        normed = (centered * lax.rsqrt(variance + EPSILON) * gain_ref[...]).astype(BF16)
        gate_up = dot(normed, gate_up_ref[...])
        gate, up = gate_up[:, :hid], gate_up[:, hid:]
        hidden = (0.5 * gate * (1.0 + jnp.tanh(0.5 * gate)) * up).astype(BF16)
        value = value + dot(hidden, down_ref[...])
        for n, (q, at) in enumerate(block):
            rows_here = at.stop - at.start
            start[q, at] = value[n * rows_here : (n + 1) * rows_here]
    result = [start[q].astype(BF16) for q in range(2)]
    for p in range(pairs):
        for q in range(2):
            pair_out[2 * p + q] = result[q][p * size : (p + 1) * size]
    dist = lax.dot_general(
        jnp.concatenate(result, axis=1), distance_ref[...], NT, preferred_element_type=F32
    ).astype(BF16)
    for p in range(pairs):
        dist_out[:, 2 * p * bins : 2 * (p + 1) * bins] = dist[p * size : (p + 1) * size]


def own_kernel(*refs):
    count = len(PARTS)
    pairs_in, dists = refs[:count], refs[count : 2 * count]
    pair_out, own_ref, sems = refs[2 * count :]
    targets = []
    length = pair_out.shape[0]
    for (k, eighth, _), part in zip(PARTS, pairs_in, strict=True):
        rows, size, _ = part.shape
        targets.append(pair_out.at[pl.ds(eighth * length // 8, rows), pl.ds(half_of("row", k, size), size)])
    copies = fetch(pairs_in, targets, sems)
    lanes = own_ref.shape[2]
    for (k, eighth, _), part, dist in zip(PARTS, pairs_in, dists, strict=True):
        rows, size, _ = part.shape
        pairs = rows // 2
        above = eighth * length // 8
        low = iota((pairs, lanes), 1) < lanes // 2
        first = half_of("row", k, size // 2)
        tiles = jnp.stack([dist[:, p * lanes : (p + 1) * lanes].astype(F32) for p in range(pairs)])
        turned = jnp.swapaxes(tiles, 0, 1)
        for j in range(0, size, 2):
            one, two = turned[j], turned[j + 1]
            own_ref[first + j // 2, pl.ds(above, pairs, stride=2), :] = jnp.where(
                low, one, pltpu.roll(two, lanes // 2, 1)
            )
            own_ref[first + j // 2, pl.ds(above + 1, pairs, stride=2), :] = jnp.where(
                low, pltpu.roll(one, lanes // 2, 1), two
            )
    for copy in copies:
        copy.wait()


def final_kernel(own_ref, bias_ref, *refs):
    out_ref = refs[len(PARTS)]
    lanes = bias_ref.shape[1]

    def write(swapped):
        for (k, eighth, _), part in zip(PARTS, refs, strict=False):
            size, width = part.shape
            first = (k + swapped) % 2 * size
            rows = slice(first, first + size)
            for t in range(width // lanes):
                tile = eighth * out_ref.shape[1] // (8 * lanes) + t
                value = own_ref[tile, rows, :] + part[:, t * lanes : (t + 1) * lanes].astype(F32) + bias_ref[...]
                out_ref[rows, tile * lanes : (tile + 1) * lanes] = value.astype(BF16)

    half = lax.axis_index("col") // (lax.axis_size("col") // 2)
    pl.when(half == 0)(functools.partial(write, 0))
    pl.when(half == 1)(functools.partial(write, 1))


PAIR_COST = pl.CostEstimate(flops=5_000_000_000, bytes_accessed=16_000_000, transcendentals=0)
COST = pl.CostEstimate(flops=0, bytes_accessed=0, transcendentals=0)


def params(mib):
    return pltpu.CompilerParams(vmem_limit_bytes=mib * MIB)


def in_hbm(*arrays):
    return [pltpu.with_memory_space_constraint(a, pltpu.HBM) for a in arrays]


VMEM = pl.BlockSpec(memory_space=pltpu.VMEM)
HBM = pl.BlockSpec(memory_space=pltpu.HBM)


def local(
    row_count,
    col_count,
    pair_state,
    token_kinds,
    first_type_table,
    second_type_table,
    alignment_state,
    alignment_index,
    alignment_table,
    first_weight,
    second_weight,
    outer_product_weight,
    outer_product_bias,
    pair_block_mask,
    transition_gain,
    transition_gate_up,
    transition_down,
    distance_weight,
    distance_bias,
):
    length = pair_state.shape[0]
    channels = pair_state.shape[2]
    depth = alignment_index.shape[0]
    features, c_width = first_weight.shape
    e_width = second_weight.shape[1]
    bins = distance_weight.shape[1]
    axes = ("row", "col")
    size = col_count // 2

    def moved(value, target):
        pairs = [
            (r * col_count + c, target(r, c)[0] * col_count + target(r, c)[1])
            for r in range(row_count)
            for c in range(col_count)
        ]
        return lax.ppermute(value, axes, pairs)

    def neighbour(value, k):
        return moved(value, lambda r, c: (r, c - c % size + (c - k) % size))

    turned_index = alignment_index.T
    other_indices = [neighbour(turned_index, k) for k in range(1, size)]
    other_states = [neighbour(alignment_state, k) for k in range(1, size)]
    kinds = alignment_table.shape[0]
    group = min(alignment_index.shape[1], 256 // features)
    own_embedded, wide_table = pl.pallas_call(
        embed_own_kernel,
        out_shape=(
            jax.ShapeDtypeStruct(alignment_state.shape, BF16),
            jax.ShapeDtypeStruct((group * kinds, group * features), BF16),
        ),
        in_specs=[HBM] * 3,
        out_specs=(VMEM,) * 2,
        scratch_shapes=[
            pltpu.VMEM(alignment_state.shape, BF16),
            pltpu.VMEM(turned_index.shape, jnp.int32),
            pltpu.VMEM(alignment_table.shape, BF16),
            pltpu.SemaphoreType.DMA((3,)),
        ],
        compiler_params=params(4),
        cost_estimate=COST,
        name="embed_own",
    )(*in_hbm(alignment_state, turned_index, alignment_table))
    embedded = pl.pallas_call(
        functools.partial(embed_group_kernel, kinds, size),
        out_shape=jax.ShapeDtypeStruct((depth, size * alignment_state.shape[1]), BF16),
        in_specs=[VMEM] * (2 * size),
        out_specs=VMEM,
        compiler_params=params(4),
        cost_estimate=COST,
        name="embed_group",
    )(own_embedded, wide_table, *other_states, *other_indices)

    rights = {
        k: moved(embedded, lambda r, c, k=k: ((c - size * k) % row_count, r)) for k in (1, 0)
    }
    other = moved(embedded, lambda r, c: (r, (c + size) % col_count))

    blocks = pair_block_mask.shape[0]
    maps = jax.ShapeDtypeStruct((blocks, length, channels), F32)
    left_shape = jax.ShapeDtypeStruct((2 * depth, 2 * length * c_width), BF16)
    (
        first_rows,
        masks,
        bases,
        outer_weight,
        pair_in,
        gate_up,
        down,
        gain,
        left_weight,
        right_weight,
        turned_distance,
        last,
        left_tiles,
    ) = pl.pallas_call(
        weights_kernel,
        out_shape=(
            jax.ShapeDtypeStruct((length, channels), F32),
            maps,
            maps,
            jax.ShapeDtypeStruct((2 * c_width * e_width, 2 * channels), BF16),
            jax.ShapeDtypeStruct(pair_state.shape, BF16),
            jax.ShapeDtypeStruct(transition_gate_up.shape, BF16),
            jax.ShapeDtypeStruct(transition_down.shape, BF16),
            jax.ShapeDtypeStruct((1, channels), F32),
            jax.ShapeDtypeStruct((8 * features, 16 * c_width), BF16),
            jax.ShapeDtypeStruct((8 * e_width, 8 * features), BF16),
            jax.ShapeDtypeStruct((2 * bins, 2 * channels), BF16),
            jax.ShapeDtypeStruct((1, 2 * bins), F32),
            left_shape,
        ),
        in_specs=[HBM] * 14 + [VMEM],
        out_specs=(VMEM,) * 13,
        scratch_shapes=[
            pltpu.VMEM((1, token_kinds.shape[0]), jnp.int32),
            pltpu.VMEM(first_type_table.shape, BF16),
            pltpu.VMEM(second_type_table.shape, BF16),
            pltpu.VMEM(outer_product_weight.shape, BF16),
            pltpu.VMEM((1, channels), BF16),
            pltpu.VMEM(pair_block_mask.shape, jnp.int32),
            pltpu.VMEM(first_weight.shape, BF16),
            pltpu.VMEM(second_weight.shape, BF16),
            pltpu.VMEM((bins, channels), BF16),
            pltpu.VMEM((1, bins), F32),
            pltpu.VMEM(outer_product_weight.shape, F32),
            pltpu.VMEM((token_kinds.shape[0], channels), F32),
            pltpu.SemaphoreType.DMA((14,)),
        ],
        compiler_params=params(8),
        cost_estimate=COST,
        name="weights",
    )(
        *in_hbm(
            token_kinds.reshape(1, -1),
            first_type_table,
            second_type_table,
            outer_product_weight,
            outer_product_bias.reshape(1, -1),
            pair_block_mask,
            pair_state,
            transition_gate_up,
            transition_down,
            first_weight,
            second_weight,
            transition_gain.reshape(1, -1),
            distance_weight.T,
            distance_bias.reshape(1, -1),
        ),
        embedded,
    )

    half = length // 2
    pair_parts, dist_parts, mirror_parts = [], [], []
    left_tiles = pl.pallas_call(
        project_left_kernel,
        out_shape=left_shape,
        in_specs=[VMEM] * 3,
        out_specs=VMEM,
        input_output_aliases={2: 0},
        compiler_params=params(4),
        cost_estimate=COST,
        name="project_left",
    )(other, left_weight, left_tiles)
    for n, part in enumerate(PARTS):
        k, _, eighths = part
        rows = length * eighths // 8
        before = dist_parts[-1:]
        if n > 1:
            before = before + [crossed]
        pair_part, dist_part = pl.pallas_call(
            functools.partial(pair_kernel, part),
            out_shape=(
                jax.ShapeDtypeStruct((rows, half, channels), BF16),
                jax.ShapeDtypeStruct((half, rows * bins), BF16),
            ),
            in_specs=[VMEM] * (12 + len(before)),
            out_specs=(VMEM,) * 2,
            scratch_shapes=[
                pltpu.VMEM((e_width // 2 * half, 2 * depth), BF16),
                pltpu.VMEM((rows // 2 * half, 2 * c_width * e_width), BF16),
                pltpu.VMEM((2, rows // 2 * half, channels), F32),
            ],
            compiler_params=params(24),
            cost_estimate=PAIR_COST,
            name="pairs",
        )(
            left_tiles,
            rights[k],
            right_weight,
            pair_in,
            first_rows,
            masks,
            bases,
            gain,
            outer_weight,
            gate_up,
            down,
            turned_distance,
            *before,
        )
        pair_parts.append(pair_part)
        dist_parts.append(dist_part)
        if n == 0:
            crossed = moved(dist_part, lambda r, c: (r, (c + size) % col_count))
            mirror_parts.append(moved(crossed, lambda r, c: ((c + size) % col_count, r)))
        else:
            mirror_parts.append(moved(dist_part, lambda r, c: (c, r)))
    pair_out, own = pl.pallas_call(
        own_kernel,
        out_shape=(
            jax.ShapeDtypeStruct(pair_state.shape, BF16),
            jax.ShapeDtypeStruct((length // 2, length, 2 * bins), F32),
        ),
        in_specs=[VMEM] * (2 * len(pair_parts)),
        out_specs=(HBM, VMEM),
        scratch_shapes=[pltpu.SemaphoreType.DMA((len(pair_parts),))],
        compiler_params=params(8),
        cost_estimate=COST,
        name="own",
    )(*pair_parts, *dist_parts)
    distogram = pl.pallas_call(
        final_kernel,
        out_shape=jax.ShapeDtypeStruct((length, length * bins), BF16),
        in_specs=[VMEM] * (2 + len(mirror_parts)),
        out_specs=VMEM,
        compiler_params=params(4),
        cost_estimate=COST,
        name="final",
    )(own, last, *mirror_parts)
    return pair_out, distogram


def solution(mesh):
    split = P(("conf", "row"), "col")
    tokens = P(None, ("conf", "row", "col"))
    in_specs = (
        P(("conf", "row"), "col", None),
        P("conf"),
        P(),
        P(),
        tokens,
        tokens,
        P(),
        P(),
        P(),
        P(),
        P(),
        split,
        P(),
        P(),
        P(),
        P(),
        P(),
    )
    return jax.shard_map(
        functools.partial(local, mesh.shape["row"], mesh.shape["col"]),
        mesh=mesh,
        in_specs=in_specs,
        out_specs=(P(("conf", "row"), "col", None), split),
        check_vma=False,
    )
```
